32 devices in a mesh: grp: 2 (over y), gx: 4 (over z), gy: 4 (over x, core).
Axes of the slice: x: 2, y: 2, z: 4, core: 2. Of those that a mesh axis runs over, the one named last changes fastest.
Arguments:
- latents: bfloat16 [8, 4, 512, 128], P(('grp', 'gx'), 'gy'), parts along dimension 0, may hold values from -6 to 6
- edge_latents: bfloat16 [8, 4, 24, 256, 128], P(('grp', 'gx'), 'gy'), parts along dimension 0, may hold values from -6 to 6
- pair_send: int32 [8, 4, 24], P(('grp', 'gx'), 'gy'), parts along dimension 0, may hold values from 0 to 8, as said below
- pair_count: int32 [8, 4], P(('grp', 'gx'), 'gy'), parts along dimension 0, may hold values from 1 to 24, as said below
- edge_send: int32 [8, 4, 24, 256], P(('grp', 'gx'), 'gy'), parts along dimension 0, may hold values from 0 to 511
- edge_recv: int32 [8, 4, 24, 256], P(('grp', 'gx'), 'gy'), parts along dimension 0, may hold values from 0 to 511
- edge_w1: bfloat16 [384, 128], replicated, may hold values from -0.3125 to 0.3125
- edge_w2: bfloat16 [128, 128], replicated, may hold values from -0.5 to 0.5
- node_w1: bfloat16 [256, 128], replicated, may hold values from -0.375 to 0.375
- node_w2: bfloat16 [128, 128], replicated, may hold values from -0.5 to 0.5
- node_ct: bfloat16 [8, 4, 512, 128], P(('grp', 'gx'), 'gy'), parts along dimension 0, may hold values from -6 to 6
Outputs:
- node_out: bfloat16 [8, 4, 512, 128], P(('grp', 'gx'), 'gy'), parts along dimension 0
- node_grad: float32 [8, 4, 512, 128], P(('grp', 'gx'), 'gy'), parts along dimension 0
- grad_edge_w1: float32 [768, 128], P('grp'), parts along dimension 0
- grad_edge_w2: float32 [256, 128], P('grp'), parts along dimension 0
- grad_node_w1: float32 [512, 128], P('grp'), parts along dimension 0
- grad_node_w2: float32 [256, 128], P('grp'), parts along dimension 0
The draws below stay inside these ranges and needn't reach their ends.
There are 2 independent parts, one for each index of `grp`. The reference program is written for one: setup_inputs(seed, part) draws one part's arguments, and reference() takes and returns one part's arrays. A program takes and returns all parts, laid end to end along the dimension named above; an argument that names none is the same for every part. Nothing has to cross between parts.
Inputs may be any that keep to these rules, and one draw needn't show every extreme that they name: `pair_send`: A slot's value s names the neighbour block at offsets (s // 3 - 1, s % 3 - 1) from its own column; that block lies inside the grid. `pair_count`: slots from this count on are padding. In every draw some device column uses all 24 slots.
All inputs are finite; a program needn't handle non-finite values.
Results may differ from the reference program's by a relative error of at most 0.0079.
Values may be sent and summed in bfloat16 or wider, within the bound.
A program may use at most 64 MiB of HBM per device.

```python
import math
import jax
import jax.numpy as jnp
from jax import lax

F = 128
HID = 128
BLK = 512
EPB = 256
PAIRS = 24
NX = 4
NY = 4
NODES = 8192


def draw_pair_send(key, part):
    key = jax.random.fold_in(key, 11)
    first_key, second_key = jax.random.split(key)
    grid_shape = (NX, NY, PAIRS)
    along_x = jax.random.randint(first_key, grid_shape, 0, 3)
    along_y = jax.random.randint(second_key, grid_shape, 0, 3)
    column_x = lax.broadcasted_iota(jnp.int32, grid_shape, 0)
    column_y = lax.broadcasted_iota(jnp.int32, grid_shape, 1)
    along_x = jnp.where((column_x == 0) & (along_x == 0), 2, along_x)
    along_x = jnp.where((column_x == NX - 1) & (along_x == 2), 0, along_x)
    along_y = jnp.where((column_y == 0) & (along_y == 0), 2, along_y)
    along_y = jnp.where((column_y == NY - 1) & (along_y == 2), 0, along_y)
    return (along_x * 3 + along_y).astype(jnp.int32)


def draw_pair_count(key, part):
    key = jax.random.fold_in(key, 23)
    subkeys = jax.random.split(key, 4)
    grid_shape = (NX, NY)
    wet_rows = max(NX // 4, 1)
    column_x = lax.broadcasted_iota(jnp.int32, grid_shape, 0)
    heavy_load = jax.random.randint(subkeys[0], grid_shape, PAIRS // 2, PAIRS + 1)
    light_load = jax.random.randint(subkeys[1], grid_shape, 1, PAIRS // 4 + 1)
    counts = jnp.where(column_x < wet_rows, heavy_load, light_load)
    pick_x = jax.random.randint(subkeys[2], (), 0, wet_rows)
    pick_y = jax.random.randint(subkeys[3], (), 0, NY)
    counts = counts.at[pick_x, pick_y].set(PAIRS)
    return counts.astype(jnp.int32)


def set_ends(array, own_key, low, top_value):
    place = [jax.random.randint(jax.random.fold_in(own_key, axis), (), 0, length) for axis, length in enumerate(array.shape)]
    widest = array.shape.index(max(array.shape))
    beside = place[:widest] + [(place[widest] + 1) % array.shape[widest]] + place[widest + 1:]
    return array.at[tuple(place)].set(low).at[tuple(beside)].set(top_value)


def level_of(key, dims, cuts, low, top_value):
    loudness = 1.0
    for dim, parts in cuts:
        steps = jax.random.uniform(jax.random.fold_in(jax.random.fold_in(key, 6), dim), (parts,), jnp.float32, low / len(cuts), top_value / len(cuts))
        loudness = loudness * jnp.repeat(jnp.exp(steps), dims[dim] // parts).reshape((-1,) + (1,) * (len(dims) - 1 - dim))
    return loudness


def scatter_about(own_key, extent, spread, most, cuts=(), kind=jnp.bfloat16):
    drawn = spread * jax.random.normal(own_key, extent, jnp.float32)
    if cuts:
        drawn = drawn * level_of(own_key, extent, cuts, -0.22, 0.18)
    return jnp.clip(drawn, -most, most).astype(kind)


def setup_inputs(seed: int = 0, part: int = 0) -> dict:
    streams_of = jax.random.split(jax.random.key(seed), 12)
    part_splits = jax.random.split(jax.random.fold_in(streams_of[11], part), 12)
    latents = scatter_about(part_splits[0], (NX, NY, BLK, F), 1.0, 6.0, ((0, 4), (1, 4)))
    edge_latents = scatter_about(part_splits[1], (NX, NY, PAIRS, EPB, F), 1.0, 6.0, ((0, 4), (1, 4)))
    pair_send = draw_pair_send(jax.random.fold_in(jax.random.fold_in(streams_of[11], part), 71), part)
    pair_count = draw_pair_count(jax.random.fold_in(jax.random.fold_in(streams_of[11], part), 71), part)
    edge_send = set_ends(jax.random.randint(part_splits[4], (NX, NY, PAIRS, EPB), 0, BLK), jax.random.fold_in(part_splits[4], 1), 0, BLK - 1).astype(jnp.int32)
    edge_recv = set_ends(jax.random.randint(part_splits[5], (NX, NY, PAIRS, EPB), 0, BLK), jax.random.fold_in(part_splits[5], 1), 0, BLK - 1).astype(jnp.int32)
    edge_w1 = scatter_about(streams_of[6], (3 * F, HID), (3 * F) ** -0.5, 0.3125)
    edge_w2 = scatter_about(streams_of[7], (HID, F), HID ** -0.5, 0.5)
    node_w1 = scatter_about(streams_of[8], (2 * F, HID), (2 * F) ** -0.5, 0.375)
    node_w2 = scatter_about(streams_of[9], (HID, F), HID ** -0.5, 0.5)
    node_ct = scatter_about(part_splits[10], (NX, NY, BLK, F), 1.0, 6.0, ((0, 4), (1, 4)))
    return dict(latents=latents, edge_latents=edge_latents, pair_send=pair_send, pair_count=pair_count, edge_send=edge_send, edge_recv=edge_recv, edge_w1=edge_w1, edge_w2=edge_w2, node_w1=node_w1, node_w2=node_w2, node_ct=node_ct)


EPSILON = 1e-05

def normalize(values):
    centre = lax.optimization_barrier(jnp.mean(values, axis=-1, keepdims=True))
    shifted = values - centre
    inverse_std = lax.rsqrt(lax.optimization_barrier(jnp.mean(shifted * shifted, axis=-1, keepdims=True)) + EPSILON)
    return shifted * inverse_std

def normalize_back(values, upstream):
    centre = lax.optimization_barrier(jnp.mean(values, axis=-1, keepdims=True))
    shifted = values - centre
    inverse_std = lax.rsqrt(lax.optimization_barrier(jnp.mean(shifted * shifted, axis=-1, keepdims=True)) + EPSILON)
    normed = shifted * inverse_std
    return inverse_std * (upstream - lax.optimization_barrier(jnp.mean(upstream, axis=-1, keepdims=True)) - normed * lax.optimization_barrier(jnp.mean(upstream * normed, axis=-1, keepdims=True)))

def silu_slope(values):
    sigmoid = jax.nn.sigmoid(values)
    return sigmoid * (1.0 + values * (1.0 - sigmoid))

def contract_rows(left_side, right_side):
    return lax.dot_general(left_side, right_side, (((0,), (0,)), ((), ())), preferred_element_type=jnp.float32)

def contract_cols(left_side, right_side):
    return lax.dot_general(left_side, right_side, (((1,), (1,)), ((), ())), preferred_element_type=jnp.float32)

def edge_forward(edge_block, receivers, senders, edge_w1, edge_w2):
    stacked = jnp.concatenate([edge_block, receivers, senders], axis=-1)
    first_pre = jnp.dot(stacked, edge_w1, preferred_element_type=jnp.float32)
    first_act = jax.nn.silu(first_pre).astype(jnp.bfloat16)
    second_pre = jnp.dot(first_act, edge_w2, preferred_element_type=jnp.float32)
    return (stacked, first_pre, first_act, second_pre)

def edge_backward(stacked, first_pre, first_act, second_pre, upstream, edge_w1, edge_w2):
    feature_width = edge_w2.shape[1]
    grad_second = normalize_back(second_pre, upstream.astype(jnp.float32)).astype(jnp.bfloat16)
    slot_w2 = contract_rows(first_act, grad_second)
    grad_first = (contract_cols(grad_second, edge_w2) * silu_slope(first_pre)).astype(jnp.bfloat16)
    slot_w1 = contract_rows(stacked, grad_first)
    grad_inputs = contract_cols(grad_first, edge_w1[feature_width:]).astype(jnp.bfloat16)
    return (slot_w1, slot_w2, grad_inputs[:, :feature_width], grad_inputs[:, feature_width:])

def node_forward(latent_rows, aggregate, node_w1, node_w2):
    stacked = jnp.concatenate([latent_rows, aggregate], axis=-1)
    first_pre = jnp.dot(stacked, node_w1, preferred_element_type=jnp.float32)
    first_act = jax.nn.silu(first_pre).astype(jnp.bfloat16)
    second_pre = jnp.dot(first_act, node_w2, preferred_element_type=jnp.float32)
    updated = (latent_rows.astype(jnp.float32) + normalize(second_pre)).astype(jnp.bfloat16)
    return ((stacked, first_pre, first_act, second_pre), updated)

def node_backward(saved_parts, cotangent, node_w1, node_w2):
    stacked, first_pre, first_act, second_pre = saved_parts
    feature_width = node_w2.shape[1]
    upstream = cotangent.astype(jnp.float32)
    grad_second = normalize_back(second_pre, upstream).astype(jnp.bfloat16)
    grad_w2 = contract_rows(first_act, grad_second)
    grad_first = (contract_cols(grad_second, node_w2) * silu_slope(first_pre)).astype(jnp.bfloat16)
    grad_w1 = contract_rows(stacked, grad_first)
    grad_inputs = contract_cols(grad_first, node_w1)
    return (grad_w1, grad_w2, upstream + grad_inputs[:, :feature_width], grad_inputs[:, feature_width:].astype(jnp.bfloat16))

def reference(latents, edge_latents, pair_send, pair_count, edge_send, edge_recv, edge_w1, edge_w2, node_w1, node_w2, node_ct):
    padded = jnp.pad(latents, ((1, 1), (1, 1), (0, 0), (0, 0)))
    zero_index = jnp.zeros((), jnp.int32)

    def neighbourhood(device):
        across = (device // NY).astype(jnp.int32)
        within = (device % NY).astype(jnp.int32)
        beside_all = lax.dynamic_slice(padded, (across, within, zero_index, zero_index), (3, 3, BLK, F))
        return (across, within, beside_all.reshape(9 * BLK, F))

    def slot_inputs(across, within, beside_all, slot_index):
        first_row = (pair_send[across, within, slot_index] * BLK).astype(jnp.int32)
        sender_block = lax.dynamic_slice_in_dim(beside_all, first_row, BLK, 0)
        senders = jnp.take(sender_block, edge_send[across, within, slot_index], axis=0)
        receivers = jnp.take(beside_all[4 * BLK:5 * BLK], edge_recv[across, within, slot_index], axis=0)
        return edge_forward(edge_latents[across, within, slot_index], receivers, senders, edge_w1, edge_w2)

    def device_gather(device):
        across, within, beside_all = neighbourhood(device)

        def forward_slot(slot_index, gathered):
            outputs = slot_inputs(across, within, beside_all, slot_index)
            message = lax.optimization_barrier(normalize(outputs[3]).astype(jnp.bfloat16)).astype(jnp.float32)
            return gathered + jax.ops.segment_sum(message, edge_recv[across, within, slot_index], num_segments=BLK)
        return lax.fori_loop(0, pair_count[across, within], forward_slot, jnp.zeros((BLK, F), jnp.float32))
    devices = jnp.arange(NX * NY, dtype=jnp.int32)
    gathered = lax.map(device_gather, devices)
    flat_rows = latents.reshape(NX * NY * BLK, F)
    node_saved, updated = node_forward(flat_rows, gathered.reshape(NX * NY * BLK, F).astype(jnp.bfloat16), node_w1, node_w2)
    grad_nw1, grad_nw2, grad_self, grad_aggregate = node_backward(node_saved, node_ct.reshape(NX * NY * BLK, F), node_w1, node_w2)
    grad_aggregate = grad_aggregate.reshape(NX, NY, BLK, F)

    def device_backward(device, running):
        returned, grad_w1, grad_w2 = running
        across, within, beside_all = neighbourhood(device)
        upstream_rows = grad_aggregate[across, within]

        def backward_slot(slot_index, inner_carry):
            towards, part_w1, part_w2 = inner_carry
            outputs = slot_inputs(across, within, beside_all, slot_index)
            upstream = jnp.take(upstream_rows, edge_recv[across, within, slot_index], axis=0)
            slot_w1, slot_w2, to_receivers, to_senders = edge_backward(outputs[0], outputs[1], outputs[2], outputs[3], upstream, edge_w1, edge_w2)
            targets = (pair_send[across, within, slot_index] * BLK + edge_send[across, within, slot_index]).astype(jnp.int32)
            towards = towards + jax.ops.segment_sum(to_senders.astype(jnp.float32), targets, num_segments=9 * BLK)
            home = (4 * BLK + edge_recv[across, within, slot_index]).astype(jnp.int32)
            towards = towards + jax.ops.segment_sum(to_receivers.astype(jnp.float32), home, num_segments=9 * BLK)
            return (towards, part_w1 + slot_w1, part_w2 + slot_w2)
        towards, grad_w1, grad_w2 = lax.fori_loop(0, pair_count[across, within], backward_slot, (jnp.zeros((9 * BLK, F), jnp.float32), grad_w1, grad_w2))
        corner = (across, within, zero_index, zero_index)
        window = lax.dynamic_slice(returned, corner, (3, 3, BLK, F))
        returned = lax.dynamic_update_slice(returned, window + towards.reshape(3, 3, BLK, F), corner)
        return (returned, grad_w1, grad_w2)
    start_state = (jnp.zeros((NX + 2, NY + 2, BLK, F), jnp.float32), jnp.zeros((3 * F, HID), jnp.float32), jnp.zeros((HID, F), jnp.float32))
    returned, grad_w1, grad_w2 = lax.fori_loop(0, NX * NY, device_backward, start_state)
    node_grad = grad_self.reshape(NX, NY, BLK, F) + returned[1:-1, 1:-1]
    factor = 1.0 / math.sqrt(NODES)
    return (updated.reshape(NX, NY, BLK, F), node_grad, grad_w1 * factor, grad_w2 * factor, grad_nw1 * factor, grad_nw2 * factor)
```

```python
import functools
import math

import jax
import jax.numpy as jnp
from jax import lax
from jax.experimental import pallas as pl
from jax.experimental.pallas import tpu as pltpu
from jax.sharding import PartitionSpec as P

EPSILON = 1e-05
UNROLL = 2


def nn(a, b):
    return lax.dot_general(a, b, (((1,), (0,)), ((), ())), preferred_element_type=jnp.float32)


def nt(a, b):
    return lax.dot_general(a, b, (((1,), (1,)), ((), ())), preferred_element_type=jnp.float32)


def moments(values):
    centre = jnp.mean(values, axis=0, keepdims=True)
    shifted = values - centre
    inverse_std = lax.rsqrt(jnp.mean(shifted * shifted, axis=0, keepdims=True) + EPSILON)
    return shifted * inverse_std, inverse_std


def norm_back(normed, inverse_std, upstream):
    return inverse_std * (
        upstream
        - jnp.mean(upstream, axis=0, keepdims=True)
        - normed * jnp.mean(upstream * normed, axis=0, keepdims=True)
    )


def local_kernel(
    send_ref, count_ref, around_ref, edges_ref, sidx_ref, ridx_ref,
    w1_ref, w2_ref, nw1_ref, nw2_ref, own_ref, ct_ref,
    out_ref, self_ref, piece_ref, g1_ref, g2_ref, gn1_ref, gn2_ref,
    slope_s, act_s, hat_s, inv_s, w1t_s, agg_s, gagg_s, gr_s, gs_s, g1a_s,
):
    f32, b16 = jnp.float32, jnp.bfloat16
    slots, width = sidx_ref.shape
    features, rows = around_ref.shape[1:]
    count = count_ref[0]
    steps = lax.div(count + (UNROLL - 1), UNROLL)

    w1t_s[...] = w1_ref[...].astype(f32).T.astype(b16)
    w2t = w2_ref[...].astype(f32).T.astype(b16)
    agg_s[...] = jnp.zeros_like(agg_s)
    gr_s[...] = jnp.zeros_like(gr_s)
    gs_s[...] = jnp.zeros_like(gs_s)
    g1a_s[...] = jnp.zeros_like(g1a_s)
    g2_ref[...] = jnp.zeros_like(g2_ref)

    def place(index_ref, step, limit):
        parts = []
        for u in range(UNROLL):
            k = step * UNROLL + u
            index = index_ref[pl.ds(k, 1), :]
            if limit:
                index = jnp.where(k < count, index, rows)
            parts.append(index)
        index = jnp.concatenate(parts, axis=1)
        spot = lax.broadcasted_iota(jnp.int32, (rows, UNROLL * width), 0)
        return (spot == index).astype(f32).astype(b16)

    def forward(step, carry):
        at_recv = place(ridx_ref, step, True)
        at_send = place(sidx_ref, step, False)
        receivers = nn(around_ref[4], at_recv).astype(b16)
        senders = jnp.concatenate(
            [
                nn(
                    around_ref[send_ref[step * UNROLL + u]],
                    at_send[:, u * width : (u + 1) * width],
                ).astype(b16)
                for u in range(UNROLL)
            ],
            axis=1,
        )
        edge = edges_ref[pl.ds(step * UNROLL, UNROLL)].reshape(UNROLL * width, features)
        pre = nt(w1t_s[:, :features], edge) + nn(
            w1t_s[:, features:], jnp.concatenate([receivers, senders], axis=0)
        )
        sigmoid = 1.0 / (1.0 + jnp.exp(-pre))
        act = (pre * sigmoid).astype(b16)
        slope_s[step] = sigmoid * (1.0 + pre * (1.0 - sigmoid))
        act_s[step] = act
        normed, inverse_std = moments(nn(w2t, act))
        hat_s[step] = normed
        inv_s[step] = inverse_std
        agg_s[...] += nt(normed.astype(b16), at_recv)
        return carry

    lax.fori_loop(0, steps, forward, 0)

    own = around_ref[4]
    stacked = jnp.concatenate([own, agg_s[...].astype(b16)], axis=0)
    nw1t = nw1_ref[...].astype(f32).T.astype(b16)
    nw2t = nw2_ref[...].astype(f32).T.astype(b16)
    pre = nn(nw1t, stacked)
    sigmoid = 1.0 / (1.0 + jnp.exp(-pre))
    act = (pre * sigmoid).astype(b16)
    slope = sigmoid * (1.0 + pre * (1.0 - sigmoid))
    normed, inverse_std = moments(nn(nw2t, act))
    out_ref[...] = (own_ref[...].astype(f32) + normed.T).astype(b16)
    upstream = ct_ref[...].astype(f32).T
    grad_second = norm_back(normed, inverse_std, upstream).astype(b16)
    gn2_ref[...] = nt(act, grad_second)
    grad_first = (nn(nw2_ref[...], grad_second) * slope).astype(b16)
    gn1_ref[...] = nt(stacked, grad_first)
    grad_inputs = nn(nw1_ref[...], grad_first)
    self_ref[...] = upstream + grad_inputs[:features]
    gagg_s[...] = grad_inputs[features:].astype(b16)

    def backward(step, carry):
        at_recv = place(ridx_ref, step, True)
        at_send = place(sidx_ref, step, False)
        upstream = nn(gagg_s[...], at_recv)
        act = act_s[step]
        grad_second = norm_back(hat_s[step], inv_s[step], upstream).astype(b16)
        g2_ref[...] += nt(act, grad_second)
        grad_first = (nn(w2_ref[...], grad_second) * slope_s[step]).astype(b16)
        edge = edges_ref[pl.ds(step * UNROLL, UNROLL)].reshape(UNROLL * width, features)
        g1a_s[...] += nn(grad_first, edge)
        gr_s[...] += nt(grad_first, at_recv)
        for u in range(UNROLL):
            part = slice(u * width, (u + 1) * width)
            gs_s[send_ref[step * UNROLL + u]] += nt(grad_first[:, part], at_send[:, part])
        return carry

    lax.fori_loop(0, steps, backward, 0)

    to_recv = gr_s[...].astype(b16)
    g1_ref[:features] = g1a_s[...].T
    g1_ref[features : 2 * features] = nt(own, to_recv)
    self_ref[...] += nn(w1_ref[features : 2 * features], to_recv)
    total = jnp.zeros((features, features), f32)
    for b in range(9):
        to_send = gs_s[b].astype(b16)
        total += nt(around_ref[b], to_send)
        piece_ref[b] = nn(w1_ref[2 * features :], to_send).astype(b16)
    g1_ref[2 * features :] = total
    self_ref[...] += nn(w1_ref[2 * features :], gs_s[4].astype(b16))


def run_local(send, count, around, edges, sidx, ridx, w1, w2, nw1, nw2, own, ct):
    f32, b16 = jnp.float32, jnp.bfloat16
    rows, features = own.shape
    slots, width = sidx.shape
    steps = slots // UNROLL
    wide = UNROLL * width
    smem = pl.BlockSpec(memory_space=pltpu.SMEM)
    vmem = pl.BlockSpec(memory_space=pltpu.VMEM)
    shape = jax.ShapeDtypeStruct
    return pl.pallas_call(
        local_kernel,
        in_specs=[smem, smem] + [vmem] * 10,
        out_specs=[vmem] * 7,
        out_shape=[
            shape((rows, features), b16),
            shape((features, rows), f32),
            shape((9, features, rows), b16),
            shape((3 * features, features), f32),
            shape((features, features), f32),
            shape((2 * features, features), f32),
            shape((features, features), f32),
        ],
        scratch_shapes=[
            pltpu.VMEM((steps, features, wide), f32),
            pltpu.VMEM((steps, features, wide), b16),
            pltpu.VMEM((steps, features, wide), f32),
            pltpu.VMEM((steps, 1, wide), f32),
            pltpu.VMEM((features, 3 * features), b16),
            pltpu.VMEM((features, rows), f32),
            pltpu.VMEM((features, rows), b16),
            pltpu.VMEM((features, rows), f32),
            pltpu.VMEM((9, features, rows), f32),
            pltpu.VMEM((features, features), f32),
        ],
        compiler_params=pltpu.CompilerParams(vmem_limit_bytes=48 * 1024 * 1024),
    )(send, count, around, edges, sidx, ridx, w1, w2, nw1, nw2, own, ct)


def halo_permute(block):
    for axis, dim in (("gx", 0), ("gy", 1)):
        count = lax.axis_size(axis)
        forward = [(i, i + 1) for i in range(count - 1)]
        backward = [(target, source) for source, target in forward]
        low = lax.ppermute(block, axis, forward)
        high = lax.ppermute(block, axis, backward)
        block = jnp.concatenate([low, block, high], axis=dim)
    return block


def passed_along(value, axis, steps):
    count = lax.axis_size(axis)
    initial, last = (max(0, -steps), min(count, count - steps))
    return lax.ppermute(value, axis, [(source, source + steps) for source in range(initial, last)])


def return_permute(pieces, kept):
    row_span = lax.axis_size("gy")
    row_place = lax.axis_index("gy")
    incoming = kept
    for across in range(3):
        for within in range(3):
            if across != 1 or within != 1:
                shift_gx = across - 1
                shift_gy = within - 1
                arrived = passed_along(
                    pieces[3 * across + within],
                    ("gx", "gy"),
                    shift_gx * row_span + shift_gy,
                ).astype(jnp.float32)
                inside = (row_place - shift_gy >= 0) & (row_place - shift_gy < row_span)
                incoming = incoming + jnp.where(inside, arrived, 0.0)
    return incoming.T


def shards(
    latents, edge_latents, pair_send, pair_count, edge_send, edge_recv,
    edge_w1, edge_w2, node_w1, node_w2, node_ct,
):
    rows, features = latents.shape[2:]
    own = latents[0, 0]
    around = halo_permute(own.T[None, None]).reshape(9, features, rows)
    updated, kept, pieces, g1, g2, gn1, gn2 = run_local(
        pair_send[0, 0], pair_count[0], around, edge_latents[0, 0], edge_send[0, 0],
        edge_recv[0, 0], edge_w1, edge_w2, node_w1, node_w2, own, node_ct[0, 0],
    )
    node_grad = return_permute(pieces, kept)
    summed = lax.psum((g1, g2, gn1, gn2), ("gx", "gy"))
    factor = 1.0 / math.sqrt(rows * lax.axis_size("gx") * lax.axis_size("gy"))
    return (updated[None, None], node_grad[None, None]) + tuple(s * factor for s in summed)


def solution(mesh):
    block = P(("grp", "gx"), "gy")
    return jax.shard_map(
        shards,
        mesh=mesh,
        in_specs=(block,) * 6 + (P(),) * 4 + (block,),
        out_specs=(block, block) + (P("grp", None),) * 4,
        check_vma=False,
    )
```

```python
import functools
import math

import jax
import jax.numpy as jnp
from jax import lax
from jax.experimental import pallas as pl
from jax.experimental.pallas import tpu as pltpu
from jax.sharding import PartitionSpec as P

EPSILON = 1e-05
UNROLL = 2


def nn(a, b):
    return lax.dot_general(a, b, (((1,), (0,)), ((), ())), preferred_element_type=jnp.float32)


def nt(a, b):
    return lax.dot_general(a, b, (((1,), (1,)), ((), ())), preferred_element_type=jnp.float32)


def moments(values):
    centre = jnp.mean(values, axis=0, keepdims=True)
    shifted = values - centre
    inverse_std = lax.rsqrt(jnp.mean(shifted * shifted, axis=0, keepdims=True) + EPSILON)
    return shifted * inverse_std, inverse_std


def norm_back(normed, inverse_std, upstream):
    return inverse_std * (
        upstream
        - jnp.mean(upstream, axis=0, keepdims=True)
        - normed * jnp.mean(upstream * normed, axis=0, keepdims=True)
    )


def local_kernel(
    factor, send_ref, count_ref, around_ref, edges_ref, sidx_ref, ridx_ref,
    w1_ref, w2_ref, nw1_ref, nw2_ref, own_ref, ct_ref,
    out_ref, self_ref, piece_ref, grads_ref,
    slope_s, act_s, hat_s, inv_s, w1t_s, agg_s, gagg_s, gr_s, gs_s, g1a_s, g2_s,
):
    f32, b16 = jnp.float32, jnp.bfloat16
    slots, width = sidx_ref.shape
    features, rows = around_ref.shape[1:]
    count = count_ref[0]
    steps = lax.div(count + (UNROLL - 1), UNROLL)

    w1t_s[...] = w1_ref[...].astype(f32).T.astype(b16)
    w2t = w2_ref[...].astype(f32).T.astype(b16)
    agg_s[...] = jnp.zeros_like(agg_s)
    gr_s[...] = jnp.zeros_like(gr_s)
    gs_s[...] = jnp.zeros_like(gs_s)
    g1a_s[...] = jnp.zeros_like(g1a_s)
    g2_s[...] = jnp.zeros_like(g2_s)

    def place(index_ref, step, limit):
        parts = []
        for u in range(UNROLL):
            k = step * UNROLL + u
            index = index_ref[pl.ds(k, 1), :]
            if limit:
                index = jnp.where(k < count, index, rows)
            parts.append(index)
        index = jnp.concatenate(parts, axis=1)
        spot = lax.broadcasted_iota(jnp.int32, (rows, UNROLL * width), 0)
        return (spot == index).astype(f32).astype(b16)

    def forward(step, carry):
        at_recv = place(ridx_ref, step, True)
        at_send = place(sidx_ref, step, False)
        receivers = nn(around_ref[4], at_recv).astype(b16)
        senders = jnp.concatenate(
            [
                nn(
                    around_ref[send_ref[step * UNROLL + u]],
                    at_send[:, u * width : (u + 1) * width],
                ).astype(b16)
                for u in range(UNROLL)
            ],
            axis=1,
        )
        edge = edges_ref[pl.ds(step * UNROLL, UNROLL)].reshape(UNROLL * width, features)
        pre = nt(w1t_s[:, :features], edge) + nn(
            w1t_s[:, features:], jnp.concatenate([receivers, senders], axis=0)
        )
        sigmoid = 1.0 / (1.0 + jnp.exp(-pre))
        act = (pre * sigmoid).astype(b16)
        slope_s[step] = sigmoid * (1.0 + pre * (1.0 - sigmoid))
        act_s[step] = act
        normed, inverse_std = moments(nn(w2t, act))
        hat_s[step] = normed
        inv_s[step] = inverse_std
        agg_s[...] += nt(normed.astype(b16), at_recv)
        return carry

    lax.fori_loop(0, steps, forward, 0)

    own = around_ref[4]
    stacked = jnp.concatenate([own, agg_s[...].astype(b16)], axis=0)
    nw1t = nw1_ref[...].astype(f32).T.astype(b16)
    nw2t = nw2_ref[...].astype(f32).T.astype(b16)
    pre = nn(nw1t, stacked)
    sigmoid = 1.0 / (1.0 + jnp.exp(-pre))
    act = (pre * sigmoid).astype(b16)
    slope = sigmoid * (1.0 + pre * (1.0 - sigmoid))
    normed, inverse_std = moments(nn(nw2t, act))
    out_ref[...] = (own_ref[...].astype(f32) + normed.T).astype(b16)
    upstream = ct_ref[...].astype(f32).T
    grad_second = norm_back(normed, inverse_std, upstream).astype(b16)
    grads_ref[6 * features : 7 * features] = nt(act, grad_second) * factor
    grad_first = (nn(nw2_ref[...], grad_second) * slope).astype(b16)
    grads_ref[4 * features : 6 * features] = nt(stacked, grad_first) * factor
    grad_inputs = nn(nw1_ref[...], grad_first)
    self_ref[...] = upstream + grad_inputs[:features]
    gagg_s[...] = grad_inputs[features:].astype(b16)

    def backward(step, carry):
        at_recv = place(ridx_ref, step, True)
        at_send = place(sidx_ref, step, False)
        upstream = nn(gagg_s[...], at_recv)
        act = act_s[step]
        grad_second = norm_back(hat_s[step], inv_s[step], upstream).astype(b16)
        g2_s[...] += nt(act, grad_second)
        grad_first = (nn(w2_ref[...], grad_second) * slope_s[step]).astype(b16)
        edge = edges_ref[pl.ds(step * UNROLL, UNROLL)].reshape(UNROLL * width, features)
        g1a_s[...] += nn(grad_first, edge)
        gr_s[...] += nt(grad_first, at_recv)
        for u in range(UNROLL):
            part = slice(u * width, (u + 1) * width)
            gs_s[send_ref[step * UNROLL + u]] += nt(grad_first[:, part], at_send[:, part])
        return carry

    lax.fori_loop(0, steps, backward, 0)

    to_recv = gr_s[...].astype(b16)
    grads_ref[:features] = g1a_s[...].T * factor
    grads_ref[features : 2 * features] = nt(own, to_recv) * factor
    self_ref[...] += nn(w1_ref[features : 2 * features], to_recv)
    total = jnp.zeros((features, features), f32)
    for b in range(9):
        to_send = gs_s[b].astype(b16)
        total += nt(around_ref[b], to_send)
        piece_ref[b] = nn(w1_ref[2 * features :], to_send).astype(b16)
    grads_ref[2 * features : 3 * features] = total * factor
    grads_ref[3 * features : 4 * features] = g2_s[...] * factor
    if grads_ref.shape[0] > 7 * features:
        grads_ref[7 * features :] = jnp.zeros((grads_ref.shape[0] - 7 * features, features), f32)
    self_ref[...] += nn(w1_ref[2 * features :], gs_s[4].astype(b16))


def run_local(factor, padded, send, count, around, edges, sidx, ridx, w1, w2, nw1, nw2, own, ct):
    f32, b16 = jnp.float32, jnp.bfloat16
    rows, features = own.shape
    slots, width = sidx.shape
    steps = slots // UNROLL
    wide = UNROLL * width
    smem = pl.BlockSpec(memory_space=pltpu.SMEM)
    vmem = pl.BlockSpec(memory_space=pltpu.VMEM)
    shape = jax.ShapeDtypeStruct
    return pl.pallas_call(
        functools.partial(local_kernel, factor),
        in_specs=[smem, smem] + [vmem] * 10,
        out_specs=[vmem] * 4,
        out_shape=[
            shape((rows, features), b16),
            shape((features, rows), f32),
            shape((9, features, rows), b16),
            shape((padded, features), f32),
        ],
        scratch_shapes=[
            pltpu.VMEM((steps, features, wide), f32),
            pltpu.VMEM((steps, features, wide), b16),
            pltpu.VMEM((steps, features, wide), f32),
            pltpu.VMEM((steps, 1, wide), f32),
            pltpu.VMEM((features, 3 * features), b16),
            pltpu.VMEM((features, rows), f32),
            pltpu.VMEM((features, rows), b16),
            pltpu.VMEM((features, rows), f32),
            pltpu.VMEM((9, features, rows), f32),
            pltpu.VMEM((features, features), f32),
            pltpu.VMEM((features, features), f32),
        ],
        compiler_params=pltpu.CompilerParams(vmem_limit_bytes=48 * 1024 * 1024),
    )(send, count, around, edges, sidx, ridx, w1, w2, nw1, nw2, own, ct)


MESH = pl.DeviceIdType.MESH


def neighbours():
    p, q = lax.axis_index("gx"), lax.axis_index("gy")
    found = []
    for i in range(9):
        if i != 4:
            x, y = p + (i // 3 - 1), q + (i % 3 - 1)
            inside = (x >= 0) & (x < lax.axis_size("gx")) & (y >= 0) & (y < lax.axis_size("gy"))
            found.append((i, {"gx": x, "gy": y}, inside))
    return found


def greet(extra):
    barrier = pltpu.get_barrier_semaphore()
    total = jnp.int32(len(extra))
    for _, where, inside in neighbours():
        total = total + inside.astype(jnp.int32)

        @pl.when(inside)
        def _():
            pl.semaphore_signal(barrier, inc=1, device_id=where, device_id_type=MESH)

    for where in extra:
        pl.semaphore_signal(barrier, inc=1, device_id=where, device_id_type=MESH)
    pl.semaphore_wait(barrier, total)


def remote(src, dst, send_sem, recv_sem, where):
    return pltpu.make_async_remote_copy(
        src_ref=src, dst_ref=dst, send_sem=send_sem, recv_sem=recv_sem,
        device_id=where, device_id_type=MESH,
    )


def halo_kernel(own_ref, around_ref, mine_s, send_sem, recv_sem):
    mine = own_ref[...].astype(jnp.float32).T.astype(jnp.bfloat16)
    mine_s[...] = mine
    around_ref[4] = mine
    greet([])
    for i, where, inside in neighbours():

        @pl.when(inside)
        def _():
            remote(mine_s, around_ref.at[8 - i], send_sem.at[i], recv_sem.at[8 - i], where).start()

        @pl.when(jnp.logical_not(inside))
        def _():
            around_ref[i] = jnp.zeros(mine.shape, mine.dtype)

    for i, where, inside in neighbours():

        @pl.when(inside)
        def _():
            remote(mine_s, around_ref.at[i], send_sem.at[i], recv_sem.at[i], where).wait()


def run_halo(own):
    rows, features = own.shape
    vmem = pl.BlockSpec(memory_space=pltpu.VMEM)
    return pl.pallas_call(
        halo_kernel,
        in_specs=[vmem],
        out_specs=vmem,
        out_shape=jax.ShapeDtypeStruct((9, features, rows), own.dtype),
        scratch_shapes=[
            pltpu.VMEM((features, rows), own.dtype),
            pltpu.SemaphoreType.DMA((9,)),
            pltpu.SemaphoreType.DMA((9,)),
        ],
        compiler_params=pltpu.CompilerParams(collective_id=0, has_side_effects=True),
    )(own)


def tail_kernel(
    pieces_ref, kept_ref, grads_ref, node_ref, g1_ref, g2_ref, gn1_ref, gn2_ref,
    back_s, acc_s, low_s, sum_s, low2_s, row_s, col_s, full_s,
    send_h, recv_h, send_r, recv_r,
):
    f32, b16 = jnp.float32, jnp.bfloat16
    p, q = lax.axis_index("gx"), lax.axis_index("gy")
    nx, ny = lax.axis_size("gx"), lax.axis_size("gy")
    padded, features = grads_ref.shape
    big, small = padded // ny, padded // (nx * ny)
    along_y = [(d, lax.rem(q + d, ny)) for d in range(1, ny)]
    along_x = [(d, lax.rem(p + d, nx)) for d in range(1, nx)]

    low_s[...] = grads_ref[...].astype(b16)
    greet([{"gy": y} for _, y in along_y] + [{"gx": x} for _, x in along_x])

    def rows_of(ref, start, size):
        return ref.at[pl.ds(pl.multiple_of(start, size), size)]

    scatter_y = [
        remote(rows_of(low_s, y * big, big), row_s.at[d], send_r.at[0, d], recv_r.at[0, d], {"gy": y})
        for d, y in along_y
    ]
    for copy in scatter_y:
        copy.start()
    for i, where, inside in neighbours():

        @pl.when(inside)
        def _():
            remote(pieces_ref.at[i], back_s.at[8 - i], send_h.at[i], recv_h.at[8 - i], where).start()

    total = grads_ref[pl.ds(pl.multiple_of(q * big, big), big), :]
    for (d, _), copy in zip(along_y, scatter_y):
        copy.wait_recv()
        total = total + row_s[d].astype(f32)
    sum_s[...] = total
    low2_s[...] = total.astype(b16)
    scatter_x = [
        remote(rows_of(low2_s, x * small, small), col_s.at[d], send_r.at[1, d], recv_r.at[1, d], {"gx": x})
        for d, x in along_x
    ]
    for copy in scatter_x:
        copy.start()
    total = sum_s[pl.ds(pl.multiple_of(p * small, small), small), :]
    for (d, _), copy in zip(along_x, scatter_x):
        copy.wait_recv()
        total = total + col_s[d].astype(f32)
    own_rows = rows_of(full_s, q * big + p * small, small)
    own_rows[...] = total.astype(b16)
    gather_x = [
        remote(own_rows, own_rows, send_r.at[2, d], recv_r.at[2, d], {"gx": x}) for d, x in along_x
    ]
    for copy in gather_x:
        copy.start()
    for d, _ in along_x:
        source = lax.rem(p + nx - d, nx)
        theirs = rows_of(full_s, q * big + source * small, small)
        remote(theirs, theirs, send_r.at[2, d], recv_r.at[2, d], {"gx": source}).wait_recv()
    for copy in gather_x:
        copy.wait_send()
    own_big = rows_of(full_s, q * big, big)
    gather_y = [
        remote(own_big, own_big, send_r.at[3, d], recv_r.at[3, d], {"gy": y}) for d, y in along_y
    ]
    for copy in gather_y:
        copy.start()

    acc_s[...] = kept_ref[...]
    for i, where, inside in neighbours():

        @pl.when(inside)
        def _():
            remote(pieces_ref.at[i], back_s.at[i], send_h.at[i], recv_h.at[i], where).wait()
            acc_s[...] += back_s[i].astype(f32)

    node_ref[...] = acc_s[...].T
    for d, _ in along_y:
        source = lax.rem(q + ny - d, ny)
        theirs = rows_of(full_s, source * big, big)
        remote(theirs, theirs, send_r.at[3, d], recv_r.at[3, d], {"gy": source}).wait_recv()
    g1_ref[...] = full_s[: 3 * features].astype(f32)
    g2_ref[...] = full_s[3 * features : 4 * features].astype(f32)
    gn1_ref[...] = full_s[4 * features : 6 * features].astype(f32)
    gn2_ref[...] = full_s[6 * features : 7 * features].astype(f32)
    for copy in scatter_y + scatter_x + gather_y:
        copy.wait_send()


def run_tail(pieces, kept, grads):
    f32, b16 = jnp.float32, jnp.bfloat16
    features, rows = kept.shape
    nx, ny = lax.axis_size("gx"), lax.axis_size("gy")
    padded = grads.shape[0]
    big, small = padded // ny, padded // (nx * ny)
    vmem = pl.BlockSpec(memory_space=pltpu.VMEM)
    shape = jax.ShapeDtypeStruct
    return pl.pallas_call(
        tail_kernel,
        in_specs=[vmem] * 3,
        out_specs=[vmem] * 5,
        out_shape=[shape((rows, features), f32)]
        + [shape((n * features, features), f32) for n in (3, 1, 2, 1)],
        scratch_shapes=[
            pltpu.VMEM((9, features, rows), b16),
            pltpu.VMEM((features, rows), f32),
            pltpu.VMEM((padded, features), b16),
            pltpu.VMEM((big, features), f32),
            pltpu.VMEM((big, features), b16),
            pltpu.VMEM((ny, big, features), b16),
            pltpu.VMEM((nx, small, features), b16),
            pltpu.VMEM((padded, features), b16),
            pltpu.SemaphoreType.DMA((9,)),
            pltpu.SemaphoreType.DMA((9,)),
            pltpu.SemaphoreType.DMA((4, max(nx, ny))),
            pltpu.SemaphoreType.DMA((4, max(nx, ny))),
        ],
        compiler_params=pltpu.CompilerParams(
            collective_id=1, has_side_effects=True, vmem_limit_bytes=32 * 1024 * 1024
        ),
    )(pieces, kept, grads)


def passed_along(value, axis, steps):
    count = lax.axis_size(axis)
    initial, last = (max(0, -steps), min(count, count - steps))
    return lax.ppermute(value, axis, [(source, source + steps) for source in range(initial, last)])


def return_permute(pieces, kept):
    row_span = lax.axis_size("gy")
    row_place = lax.axis_index("gy")
    incoming = kept
    for across in range(3):
        for within in range(3):
            if across != 1 or within != 1:
                shift_gx = across - 1
                shift_gy = within - 1
                arrived = passed_along(
                    pieces[3 * across + within],
                    ("gx", "gy"),
                    shift_gx * row_span + shift_gy,
                ).astype(jnp.float32)
                inside = (row_place - shift_gy >= 0) & (row_place - shift_gy < row_span)
                incoming = incoming + jnp.where(inside, arrived, 0.0)
    return incoming.T


def shards(
    latents, edge_latents, pair_send, pair_count, edge_send, edge_recv,
    edge_w1, edge_w2, node_w1, node_w2, node_ct,
):
    rows, features = latents.shape[2:]
    own = latents[0, 0]
    around = run_halo(own)
    nx, ny = lax.axis_size("gx"), lax.axis_size("gy")
    factor = 1.0 / math.sqrt(rows * nx * ny)
    direct = nx * ny <= 16
    unit = 16 * nx * ny if direct else 1
    padded = -(-7 * features // unit) * unit
    updated, kept, pieces, grads = run_local(
        factor, padded, pair_send[0, 0], pair_count[0], around, edge_latents[0, 0],
        edge_send[0, 0], edge_recv[0, 0], edge_w1, edge_w2, node_w1, node_w2, own, node_ct[0, 0],
    )
    if direct:
        node_grad, *summed = run_tail(pieces, kept, grads)
    else:
        node_grad = return_permute(pieces, kept)
        grads = lax.psum(grads, ("gx", "gy"))
        summed = jnp.split(grads, (3 * features, 4 * features, 6 * features))
    return (updated[None, None], node_grad[None, None]) + tuple(summed)


def solution(mesh):
    block = P(("grp", "gx"), "gy")
    return jax.shard_map(
        shards,
        mesh=mesh,
        in_specs=(block,) * 6 + (P(),) * 4 + (block,),
        out_specs=(block, block) + (P("grp", None),) * 4,
        check_vma=False,
    )
```

```python
import functools
import math

import jax
import jax.numpy as jnp
from jax import lax
from jax.experimental import pallas as pl
from jax.experimental.pallas import tpu as pltpu
from jax.sharding import PartitionSpec as P

EPSILON = 1e-05
UNROLL = 4


def nn(a, b):
    return lax.dot_general(a, b, (((1,), (0,)), ((), ())), preferred_element_type=jnp.float32)


def nt(a, b):
    return lax.dot_general(a, b, (((1,), (1,)), ((), ())), preferred_element_type=jnp.float32)


def moments(values):
    centre = jnp.mean(values, axis=0, keepdims=True)
    shifted = values - centre
    inverse_std = lax.rsqrt(jnp.mean(shifted * shifted, axis=0, keepdims=True) + EPSILON)
    return shifted * inverse_std, inverse_std


def norm_back(normed, inverse_std, upstream):
    return inverse_std * (
        upstream
        - jnp.mean(upstream, axis=0, keepdims=True)
        - normed * jnp.mean(upstream * normed, axis=0, keepdims=True)
    )


def local_kernel(
    factor, send_ref, count_ref, around_hbm, edges_hbm, sidx_ref, ridx_ref,
    w1_ref, w2_ref, nw1_ref, nw2_ref, own_ref, ct_ref,
    out_ref, self_ref, piece_ref, grads_ref,
    slope_s, act_s, hat_s, inv_s, w1t_s, agg_s, gagg_s, gr_s, gs_s, g1a_s, g2_s,
    around_ref, edges_ref, fetch_sem,
):
    f32, b16 = jnp.float32, jnp.bfloat16
    fetch_around = pltpu.make_async_copy(around_hbm, around_ref, fetch_sem.at[0])
    fetch_around.start()
    fetch_edges = pltpu.make_async_copy(edges_hbm, edges_ref, fetch_sem.at[1])
    fetch_edges.start()
    slots, width = sidx_ref.shape
    features, rows = around_ref.shape[1:]
    count = count_ref[0]
    steps = lax.div(count + (UNROLL - 1), UNROLL)

    w1t_s[...] = w1_ref[...].astype(f32).T.astype(b16)
    w2t = w2_ref[...].astype(f32).T.astype(b16)
    agg_s[...] = jnp.zeros_like(agg_s)
    gr_s[...] = jnp.zeros_like(gr_s)
    gs_s[...] = jnp.zeros_like(gs_s)
    g1a_s[...] = jnp.zeros_like(g1a_s)
    g2_s[...] = jnp.zeros_like(g2_s)
    fetch_around.wait()
    fetch_edges.wait()

    def place(index_ref, step, limit):
        parts = []
        for u in range(UNROLL):
            k = step * UNROLL + u
            index = index_ref[pl.ds(k, 1), :]
            if limit:
                index = jnp.where(k < count, index, rows)
            parts.append(index)
        index = jnp.concatenate(parts, axis=1)
        spot = lax.broadcasted_iota(jnp.int32, (rows, UNROLL * width), 0)
        return (spot == index).astype(f32).astype(b16)

    def forward(step, carry):
        at_recv = place(ridx_ref, step, True)
        at_send = place(sidx_ref, step, False)
        receivers = nn(around_ref[4], at_recv).astype(b16)
        senders = jnp.concatenate(
            [
                nn(
                    around_ref[send_ref[step * UNROLL + u]],
                    at_send[:, u * width : (u + 1) * width],
                ).astype(b16)
                for u in range(UNROLL)
            ],
            axis=1,
        )
        edge = edges_ref[pl.ds(step * UNROLL, UNROLL)].reshape(UNROLL * width, features)
        pre = nt(w1t_s[:, :features], edge) + nn(
            w1t_s[:, features:], jnp.concatenate([receivers, senders], axis=0)
        )
        sigmoid = 1.0 / (1.0 + jnp.exp(-pre))
        act = (pre * sigmoid).astype(b16)
        slope_s[step] = sigmoid * (1.0 + pre * (1.0 - sigmoid))
        act_s[step] = act
        normed, inverse_std = moments(nn(w2t, act))
        hat_s[step] = normed
        inv_s[step] = inverse_std
        agg_s[...] += nt(normed.astype(b16), at_recv)
        return carry

    lax.fori_loop(0, steps, forward, 0)

    own = around_ref[4]
    stacked = jnp.concatenate([own, agg_s[...].astype(b16)], axis=0)
    nw1t = nw1_ref[...].astype(f32).T.astype(b16)
    nw2t = nw2_ref[...].astype(f32).T.astype(b16)
    pre = nn(nw1t, stacked)
    sigmoid = 1.0 / (1.0 + jnp.exp(-pre))
    act = (pre * sigmoid).astype(b16)
    slope = sigmoid * (1.0 + pre * (1.0 - sigmoid))
    normed, inverse_std = moments(nn(nw2t, act))
    out_ref[...] = (own_ref[...].astype(f32) + normed.T).astype(b16)
    upstream = ct_ref[...].astype(f32).T
    grad_second = norm_back(normed, inverse_std, upstream).astype(b16)
    grads_ref[6 * features : 7 * features] = nt(act, grad_second) * factor
    grad_first = (nn(nw2_ref[...], grad_second) * slope).astype(b16)
    grads_ref[4 * features : 6 * features] = nt(stacked, grad_first) * factor
    grad_inputs = nn(nw1_ref[...], grad_first)
    self_ref[...] = upstream + grad_inputs[:features]
    gagg_s[...] = grad_inputs[features:].astype(b16)

    def backward(step, carry):
        at_recv = place(ridx_ref, step, True)
        at_send = place(sidx_ref, step, False)
        upstream = nn(gagg_s[...], at_recv)
        act = act_s[step]
        grad_second = norm_back(hat_s[step], inv_s[step], upstream).astype(b16)
        g2_s[...] += nt(act, grad_second)
        grad_first = (nn(w2_ref[...], grad_second) * slope_s[step]).astype(b16)
        edge = edges_ref[pl.ds(step * UNROLL, UNROLL)].reshape(UNROLL * width, features)
        g1a_s[...] += nn(grad_first, edge)
        gr_s[...] += nt(grad_first, at_recv)
        for u in range(UNROLL):
            part = slice(u * width, (u + 1) * width)
            gs_s[send_ref[step * UNROLL + u]] += nt(grad_first[:, part], at_send[:, part])
        return carry

    lax.fori_loop(0, steps, backward, 0)

    to_recv = gr_s[...].astype(b16)
    grads_ref[:features] = g1a_s[...].T * factor
    grads_ref[features : 2 * features] = nt(own, to_recv) * factor
    self_ref[...] += nn(w1_ref[features : 2 * features], to_recv)
    total = jnp.zeros((features, features), f32)
    for b in range(9):
        to_send = gs_s[b].astype(b16)
        total += nt(around_ref[b], to_send)
        piece_ref[b] = nn(w1_ref[2 * features :], to_send).astype(b16)
    grads_ref[2 * features : 3 * features] = total * factor
    grads_ref[3 * features : 4 * features] = g2_s[...] * factor
    if grads_ref.shape[0] > 7 * features:
        grads_ref[7 * features :] = jnp.zeros((grads_ref.shape[0] - 7 * features, features), f32)
    self_ref[...] += nn(w1_ref[2 * features :], gs_s[4].astype(b16))


def run_local(factor, padded, send, count, around, edges, sidx, ridx, w1, w2, nw1, nw2, own, ct):
    f32, b16 = jnp.float32, jnp.bfloat16
    rows, features = own.shape
    slots, width = sidx.shape
    steps = slots // UNROLL
    wide = UNROLL * width
    smem = pl.BlockSpec(memory_space=pltpu.SMEM)
    vmem = pl.BlockSpec(memory_space=pltpu.VMEM)
    shape = jax.ShapeDtypeStruct
    return pl.pallas_call(
        functools.partial(local_kernel, factor),
        in_specs=[smem, smem] + [pl.BlockSpec(memory_space=pl.ANY)] * 2 + [vmem] * 8,
        out_specs=[vmem] * 4,
        out_shape=[
            shape((rows, features), b16),
            shape((features, rows), f32),
            shape((9, features, rows), b16),
            shape((padded, features), f32),
        ],
        scratch_shapes=[
            pltpu.VMEM((steps, features, wide), f32),
            pltpu.VMEM((steps, features, wide), b16),
            pltpu.VMEM((steps, features, wide), f32),
            pltpu.VMEM((steps, 1, wide), f32),
            pltpu.VMEM((features, 3 * features), b16),
            pltpu.VMEM((features, rows), f32),
            pltpu.VMEM((features, rows), b16),
            pltpu.VMEM((features, rows), f32),
            pltpu.VMEM((9, features, rows), f32),
            pltpu.VMEM((features, features), f32),
            pltpu.VMEM((features, features), f32),
            pltpu.VMEM(around.shape, b16),
            pltpu.VMEM(edges.shape, b16),
            pltpu.SemaphoreType.DMA((2,)),
        ],
        compiler_params=pltpu.CompilerParams(vmem_limit_bytes=48 * 1024 * 1024),
    )(send, count, around, edges, sidx, ridx, w1, w2, nw1, nw2, own, ct)


MESH = pl.DeviceIdType.MESH


def position(slot):
    x = lax.axis_index("gx") + (slot // 3 - 1)
    y = lax.axis_index("gy") + (slot % 3 - 1)
    in_x = (x >= 0) & (x < lax.axis_size("gx"))
    in_y = (y >= 0) & (y < lax.axis_size("gy"))
    return x, y, in_x, in_y


def greet(extra):
    barrier = pltpu.get_barrier_semaphore()
    total = jnp.int32(len(extra))
    for slot in (1, 3, 5, 7):
        x, y, in_x, in_y = position(slot)
        inside = in_x & in_y
        total = total + inside.astype(jnp.int32)

        @pl.when(inside)
        def _():
            pl.semaphore_signal(barrier, inc=1, device_id={"gx": x, "gy": y}, device_id_type=MESH)

    for where in extra:
        pl.semaphore_signal(barrier, inc=1, device_id=where, device_id_type=MESH)
    pl.semaphore_wait(barrier, total)


def remote(src, dst, send_sem, recv_sem, where):
    return pltpu.make_async_remote_copy(
        src_ref=src, dst_ref=dst, send_sem=send_sem, recv_sem=recv_sem,
        device_id=where, device_id_type=MESH,
    )


def halo_kernel(own_ref, around_ref, send_sem, recv_sem):
    mine = own_ref[...].astype(jnp.float32).T.astype(jnp.bfloat16)
    around_ref[4] = mine
    for slot in range(9):
        if slot != 4:
            _, _, in_x, in_y = position(slot)

            @pl.when(jnp.logical_not(in_x & in_y))
            def _():
                around_ref[slot] = jnp.zeros(mine.shape, mine.dtype)

    greet([])

    def transfer(slot):
        a, b = slot // 3, slot % 3
        x, y, back_x, back_y = position(8 - slot)
        _, _, in_x, in_y = position(slot)
        if b == 1:
            source, where, sends = 4, {"gx": x}, back_x
        else:
            source, where, sends = 3 * a + 1, {"gy": y}, in_x & back_y
        copy = remote(
            around_ref.at[source], around_ref.at[slot], send_sem.at[slot], recv_sem.at[slot], where
        )
        return copy, sends, in_x & in_y

    copies = {slot: transfer(slot) for slot in range(9) if slot != 4}

    def start(*slots):
        for slot in slots:
            pl.when(copies[slot][1])(copies[slot][0].start)

    def arrived(*slots):
        for slot in slots:
            pl.when(copies[slot][2])(copies[slot][0].wait_recv)

    start(1, 7, 3, 5)
    arrived(1)
    start(0, 2)
    arrived(7)
    start(6, 8)
    arrived(3, 5, 0, 2, 6, 8)
    for copy, sends, _ in copies.values():
        pl.when(sends)(copy.wait_send)


def run_halo(own):
    rows, features = own.shape
    vmem = pl.BlockSpec(memory_space=pltpu.VMEM)
    return pl.pallas_call(
        halo_kernel,
        in_specs=[vmem],
        out_specs=vmem,
        out_shape=jax.ShapeDtypeStruct((9, features, rows), own.dtype),
        scratch_shapes=[
            pltpu.SemaphoreType.DMA((9,)),
            pltpu.SemaphoreType.DMA((9,)),
        ],
        compiler_params=pltpu.CompilerParams(collective_id=0, has_side_effects=True),
    )(own)


def tail_kernel(
    pieces_ref, kept_ref, grads_ref, acc_ref, full_s,
    back_s, pass_s, low_s, sum_s, low2_s, row_s, col_s,
    send_h, recv_h, send_r, recv_r,
):
    f32, b16 = jnp.float32, jnp.bfloat16
    p, q = lax.axis_index("gx"), lax.axis_index("gy")
    nx, ny = lax.axis_size("gx"), lax.axis_size("gy")
    padded, features = grads_ref.shape
    big, small = padded // ny, padded // (nx * ny)
    along_y = [(d, lax.rem(q + d, ny)) for d in range(1, ny)]
    along_x = [(d, lax.rem(p + d, nx)) for d in range(1, nx)]

    low_s[...] = grads_ref[...].astype(b16)
    greet([{"gy": y} for _, y in along_y] + [{"gx": x} for _, x in along_x])

    def rows_of(ref, start, size):
        return ref.at[pl.ds(pl.multiple_of(start, size), size)]

    scatter_y = [
        remote(rows_of(low_s, y * big, big), row_s.at[d], send_r.at[0, d], recv_r.at[0, d], {"gy": y})
        for d, y in along_y
    ]
    for copy in scatter_y:
        copy.start()

    def piece(slot):
        a, b = slot // 3, slot % 3
        x, y, in_x, in_y = position(slot)
        if b == 1:
            landing, source, where = 3 * (2 - a) + 1, pass_s.at[a], {"gx": x}
        else:
            landing, source, where = 3 * a + 2 - b, pieces_ref.at[slot], {"gy": y}
        copy = remote(source, back_s.at[landing], send_h.at[slot], recv_h.at[landing], where)
        return copy, in_x & in_y

    copies = {slot: piece(slot) for slot in range(9) if slot != 4}

    def take(slot):
        @pl.when(copies[slot][1])
        def _():
            x, y, _, _ = position(slot)
            sender = {"gx": x} if slot % 3 == 1 else {"gy": y}
            landed = back_s.at[slot]
            remote(landed, landed, send_h.at[slot], recv_h.at[slot], sender).wait_recv()
            acc_ref[...] += back_s[slot].astype(f32)

    for slot in (0, 2, 6, 8, 3, 5):
        pl.when(copies[slot][1])(copies[slot][0].start)

    total = grads_ref[pl.ds(pl.multiple_of(q * big, big), big), :]
    for (d, _), copy in zip(along_y, scatter_y):
        copy.wait_recv()
        total = total + row_s[d].astype(f32)
    sum_s[...] = total
    low2_s[...] = total.astype(b16)
    scatter_x = [
        remote(rows_of(low2_s, x * small, small), col_s.at[d], send_r.at[1, d], recv_r.at[1, d], {"gx": x})
        for d, x in along_x
    ]
    for copy in scatter_x:
        copy.start()
    for a in (0, 2):
        acc_ref[...] = pieces_ref[3 * a + 1].astype(f32)
        take(3 * a)
        take(3 * a + 2)
        pass_s[a] = acc_ref[...].astype(b16)
        pl.when(copies[3 * a + 1][1])(copies[3 * a + 1][0].start)
    total = sum_s[pl.ds(pl.multiple_of(p * small, small), small), :]
    for (d, _), copy in zip(along_x, scatter_x):
        copy.wait_recv()
        total = total + col_s[d].astype(f32)
    own_rows = rows_of(full_s, q * big + p * small, small)
    own_rows[...] = total.astype(b16)
    gather_x = [
        remote(own_rows, own_rows, send_r.at[2, d], recv_r.at[2, d], {"gx": x}) for d, x in along_x
    ]
    for copy in gather_x:
        copy.start()
    for d, _ in along_x:
        source = lax.rem(p + nx - d, nx)
        theirs = rows_of(full_s, q * big + source * small, small)
        remote(theirs, theirs, send_r.at[2, d], recv_r.at[2, d], {"gx": source}).wait_recv()
    for copy in gather_x:
        copy.wait_send()
    own_big = rows_of(full_s, q * big, big)
    gather_y = [
        remote(own_big, own_big, send_r.at[3, d], recv_r.at[3, d], {"gy": y}) for d, y in along_y
    ]
    for copy in gather_y:
        copy.start()

    acc_ref[...] = kept_ref[...]
    for slot in (3, 5, 1, 7):
        take(slot)
    for d, _ in along_y:
        source = lax.rem(q + ny - d, ny)
        theirs = rows_of(full_s, source * big, big)
        remote(theirs, theirs, send_r.at[3, d], recv_r.at[3, d], {"gy": source}).wait_recv()
    for copy in scatter_y + scatter_x + gather_y:
        copy.wait_send()
    for copy, sends in copies.values():
        pl.when(sends)(copy.wait_send)


def finish_kernel(acc_ref, full_ref, node_ref, g1_ref, g2_ref, gn1_ref, gn2_ref):
    node_ref[...] = acc_ref[...].T
    first = 0
    for ref in (g1_ref, g2_ref, gn1_ref, gn2_ref):
        ref[...] = full_ref[first : first + ref.shape[0]].astype(jnp.float32)
        first += ref.shape[0]


def run_finish(acc, full):
    features, rows = acc.shape
    vmem = pl.BlockSpec(memory_space=pltpu.VMEM)
    shape = jax.ShapeDtypeStruct
    return pl.pallas_call(
        finish_kernel,
        in_specs=[vmem] * 2,
        out_specs=[vmem] * 5,
        out_shape=[shape((rows, features), jnp.float32)]
        + [shape((n * features, features), jnp.float32) for n in (3, 1, 2, 1)],
    )(acc, full)


def run_tail(pieces, kept, grads):
    f32, b16 = jnp.float32, jnp.bfloat16
    features, rows = kept.shape
    nx, ny = lax.axis_size("gx"), lax.axis_size("gy")
    padded = grads.shape[0]
    big, small = padded // ny, padded // (nx * ny)
    vmem = pl.BlockSpec(memory_space=pltpu.VMEM)
    shape = jax.ShapeDtypeStruct
    return pl.pallas_call(
        tail_kernel,
        in_specs=[vmem] * 3,
        out_specs=[vmem] * 2,
        out_shape=[shape((features, rows), f32), shape((padded, features), b16)],
        scratch_shapes=[
            pltpu.VMEM((9, features, rows), b16),
            pltpu.VMEM((3, features, rows), b16),
            pltpu.VMEM((padded, features), b16),
            pltpu.VMEM((big, features), f32),
            pltpu.VMEM((big, features), b16),
            pltpu.VMEM((ny, big, features), b16),
            pltpu.VMEM((nx, small, features), b16),
            pltpu.SemaphoreType.DMA((9,)),
            pltpu.SemaphoreType.DMA((9,)),
            pltpu.SemaphoreType.DMA((4, max(nx, ny))),
            pltpu.SemaphoreType.DMA((4, max(nx, ny))),
        ],
        compiler_params=pltpu.CompilerParams(
            collective_id=1, has_side_effects=True, vmem_limit_bytes=32 * 1024 * 1024
        ),
    )(pieces, kept, grads)


def passed_along(value, axis, steps):
    count = lax.axis_size(axis)
    initial, last = (max(0, -steps), min(count, count - steps))
    return lax.ppermute(value, axis, [(source, source + steps) for source in range(initial, last)])


def return_permute(pieces, kept):
    row_span = lax.axis_size("gy")
    row_place = lax.axis_index("gy")
    incoming = kept
    for across in range(3):
        for within in range(3):
            if across != 1 or within != 1:
                shift_gx = across - 1
                shift_gy = within - 1
                arrived = passed_along(
                    pieces[3 * across + within],
                    ("gx", "gy"),
                    shift_gx * row_span + shift_gy,
                ).astype(jnp.float32)
                inside = (row_place - shift_gy >= 0) & (row_place - shift_gy < row_span)
                incoming = incoming + jnp.where(inside, arrived, 0.0)
    return incoming.T


def shards(
    latents, edge_latents, pair_send, pair_count, edge_send, edge_recv,
    edge_w1, edge_w2, node_w1, node_w2, node_ct,
):
    rows, features = latents.shape[2:]
    own = latents[0, 0]
    around = run_halo(own)
    nx, ny = lax.axis_size("gx"), lax.axis_size("gy")
    factor = 1.0 / math.sqrt(rows * nx * ny)
    direct = nx * ny <= 16
    unit = 16 * nx * ny if direct else 1
    padded = -(-7 * features // unit) * unit
    updated, kept, pieces, grads = run_local(
        factor, padded, pair_send[0, 0], pair_count[0], around, edge_latents[0, 0],
        edge_send[0, 0], edge_recv[0, 0], edge_w1, edge_w2, node_w1, node_w2, own, node_ct[0, 0],
    )
    if direct:
        node_grad, *summed = run_finish(*run_tail(pieces, kept, grads))
    else:
        node_grad = return_permute(pieces, kept)
        grads = lax.psum(grads, ("gx", "gy"))
        summed = jnp.split(grads, (3 * features, 4 * features, 6 * features))
    return (updated[None, None], node_grad[None, None]) + tuple(summed)


def solution(mesh):
    block = P(("grp", "gx"), "gy")
    return jax.shard_map(
        shards,
        mesh=mesh,
        in_specs=(block,) * 6 + (P(),) * 4 + (block,),
        out_specs=(block, block) + (P("grp", None),) * 4,
        check_vma=False,
    )
```

```python
import functools
import math

import jax
import jax.numpy as jnp
from jax import lax
from jax.experimental import pallas as pl
from jax.experimental.pallas import tpu as pltpu
from jax.sharding import PartitionSpec as P

EPSILON = 1e-05
UNROLL = 6


def nn(a, b):
    return lax.dot_general(a, b, (((1,), (0,)), ((), ())), preferred_element_type=jnp.float32)


def nt(a, b):
    return lax.dot_general(a, b, (((1,), (1,)), ((), ())), preferred_element_type=jnp.float32)


def moments(values):
    centre = jnp.mean(values, axis=0, keepdims=True)
    shifted = values - centre
    inverse_std = lax.rsqrt(jnp.mean(shifted * shifted, axis=0, keepdims=True) + EPSILON)
    return shifted * inverse_std, inverse_std


def norm_back(normed, inverse_std, upstream):
    return inverse_std * (
        upstream
        - jnp.mean(upstream, axis=0, keepdims=True)
        - normed * jnp.mean(upstream * normed, axis=0, keepdims=True)
    )


def local_kernel(
    factor, send_ref, count_ref, around_hbm, edges_hbm, sidx_ref, ridx_ref,
    w1_ref, w2_ref, nw1_ref, nw2_ref, own_ref, ct_ref,
    out_ref, self_ref, piece_ref, grads_ref,
    slope_s, act_s, hat_s, inv_s, w1t_s, agg_s, gagg_s, gr_s, gs_s, g1a_s, g2_s,
    around_ref, edges_ref, fetch_sem,
):
    f32, b16 = jnp.float32, jnp.bfloat16
    fetch_around = pltpu.make_async_copy(around_hbm, around_ref, fetch_sem.at[0])
    fetch_around.start()
    fetch_edges = pltpu.make_async_copy(edges_hbm, edges_ref, fetch_sem.at[1])
    fetch_edges.start()
    slots, width = sidx_ref.shape
    features, rows = around_ref.shape[1:]
    count = count_ref[0]
    steps = lax.div(count + (UNROLL - 1), UNROLL)

    w1t_s[...] = w1_ref[...].astype(f32).T.astype(b16)
    w2t = w2_ref[...].astype(f32).T.astype(b16)
    agg_s[...] = jnp.zeros_like(agg_s)
    gr_s[...] = jnp.zeros_like(gr_s)
    gs_s[...] = jnp.zeros_like(gs_s)
    g1a_s[...] = jnp.zeros_like(g1a_s)
    g2_s[...] = jnp.zeros_like(g2_s)
    fetch_around.wait()
    fetch_edges.wait()

    def place(index_ref, step, limit):
        parts = []
        for u in range(UNROLL):
            k = step * UNROLL + u
            index = index_ref[pl.ds(k, 1), :]
            if limit:
                index = jnp.where(k < count, index, rows)
            parts.append(index)
        index = jnp.concatenate(parts, axis=1)
        spot = lax.broadcasted_iota(jnp.int16, (rows, UNROLL * width), 0)
        match = spot == index.astype(jnp.int16)
        return jnp.where(match, jnp.ones((), b16), jnp.zeros((), b16))

    def forward(step, carry):
        at_recv = place(ridx_ref, step, True)
        at_send = place(sidx_ref, step, False)
        receivers = nn(around_ref[4], at_recv).astype(b16)
        senders = jnp.concatenate(
            [
                nn(
                    around_ref[send_ref[step * UNROLL + u]],
                    at_send[:, u * width : (u + 1) * width],
                ).astype(b16)
                for u in range(UNROLL)
            ],
            axis=1,
        )
        edge = edges_ref[pl.ds(step * UNROLL, UNROLL)].reshape(UNROLL * width, features)
        pre = nt(w1t_s[:, :features], edge) + nn(
            w1t_s[:, features:], jnp.concatenate([receivers, senders], axis=0)
        )
        sigmoid = 1.0 / (1.0 + jnp.exp(-pre))
        act = (pre * sigmoid).astype(b16)
        slope_s[step] = sigmoid * (1.0 + pre * (1.0 - sigmoid))
        act_s[step] = act
        normed, inverse_std = moments(nn(w2t, act))
        hat_s[step] = normed
        inv_s[step] = inverse_std
        agg_s[...] += nt(normed.astype(b16), at_recv)
        return carry

    lax.fori_loop(0, steps, forward, 0)

    own = around_ref[4]
    stacked = jnp.concatenate([own, agg_s[...].astype(b16)], axis=0)
    nw1t = nw1_ref[...].astype(f32).T.astype(b16)
    nw2t = nw2_ref[...].astype(f32).T.astype(b16)
    pre = nn(nw1t, stacked)
    sigmoid = 1.0 / (1.0 + jnp.exp(-pre))
    act = (pre * sigmoid).astype(b16)
    slope = sigmoid * (1.0 + pre * (1.0 - sigmoid))
    normed, inverse_std = moments(nn(nw2t, act))
    out_ref[...] = (own_ref[...].astype(f32) + normed.T).astype(b16)
    upstream = ct_ref[...].astype(f32).T
    grad_second = norm_back(normed, inverse_std, upstream).astype(b16)
    grads_ref[6 * features : 7 * features] = nt(act, grad_second) * factor
    grad_first = (nn(nw2_ref[...], grad_second) * slope).astype(b16)
    grads_ref[4 * features : 6 * features] = nt(stacked, grad_first) * factor
    grad_inputs = nn(nw1_ref[...], grad_first)
    self_ref[...] = upstream + grad_inputs[:features]
    gagg_s[...] = grad_inputs[features:].astype(b16)

    def backward(step, carry):
        at_recv = place(ridx_ref, step, True)
        at_send = place(sidx_ref, step, False)
        upstream = nn(gagg_s[...], at_recv)
        act = act_s[step]
        grad_second = norm_back(hat_s[step], inv_s[step], upstream).astype(b16)
        g2_s[...] += nt(act, grad_second)
        grad_first = (nn(w2_ref[...], grad_second) * slope_s[step]).astype(b16)
        edge = edges_ref[pl.ds(step * UNROLL, UNROLL)].reshape(UNROLL * width, features)
        g1a_s[...] += nn(grad_first, edge)
        gr_s[...] += nt(grad_first, at_recv)
        for u in range(UNROLL):
            part = slice(u * width, (u + 1) * width)
            gs_s[send_ref[step * UNROLL + u]] += nt(grad_first[:, part], at_send[:, part])
        return carry

    lax.fori_loop(0, steps, backward, 0)

    to_recv = gr_s[...].astype(b16)
    grads_ref[:features] = g1a_s[...].T * factor
    grads_ref[features : 2 * features] = nt(own, to_recv) * factor
    self_ref[...] += nn(w1_ref[features : 2 * features], to_recv)
    total = jnp.zeros((features, features), f32)
    for b in range(9):
        to_send = gs_s[b].astype(b16)
        total += nt(around_ref[b], to_send)
        piece_ref[b] = nn(w1_ref[2 * features :], to_send).astype(b16)
    grads_ref[2 * features : 3 * features] = total * factor
    grads_ref[3 * features : 4 * features] = g2_s[...] * factor
    if grads_ref.shape[0] > 7 * features:
        grads_ref[7 * features :] = jnp.zeros((grads_ref.shape[0] - 7 * features, features), f32)
    self_ref[...] += nn(w1_ref[2 * features :], gs_s[4].astype(b16))


def run_local(factor, padded, send, count, around, edges, sidx, ridx, w1, w2, nw1, nw2, own, ct):
    f32, b16 = jnp.float32, jnp.bfloat16
    rows, features = own.shape
    slots, width = sidx.shape
    steps = slots // UNROLL
    wide = UNROLL * width
    smem = pl.BlockSpec(memory_space=pltpu.SMEM)
    vmem = pl.BlockSpec(memory_space=pltpu.VMEM)
    shape = jax.ShapeDtypeStruct
    return pl.pallas_call(
        functools.partial(local_kernel, factor),
        in_specs=[smem, smem] + [pl.BlockSpec(memory_space=pl.ANY)] * 2 + [vmem] * 8,
        out_specs=[vmem] * 4,
        out_shape=[
            shape((rows, features), b16),
            shape((features, rows), f32),
            shape((9, features, rows), b16),
            shape((padded, features), f32),
        ],
        scratch_shapes=[
            pltpu.VMEM((steps, features, wide), f32),
            pltpu.VMEM((steps, features, wide), b16),
            pltpu.VMEM((steps, features, wide), f32),
            pltpu.VMEM((steps, 1, wide), f32),
            pltpu.VMEM((features, 3 * features), b16),
            pltpu.VMEM((features, rows), f32),
            pltpu.VMEM((features, rows), b16),
            pltpu.VMEM((features, rows), f32),
            pltpu.VMEM((9, features, rows), f32),
            pltpu.VMEM((features, features), f32),
            pltpu.VMEM((features, features), f32),
            pltpu.VMEM(around.shape, b16),
            pltpu.VMEM(edges.shape, b16),
            pltpu.SemaphoreType.DMA((2,)),
        ],
        compiler_params=pltpu.CompilerParams(vmem_limit_bytes=60 * 1024 * 1024),
    )(send, count, around, edges, sidx, ridx, w1, w2, nw1, nw2, own, ct)


MESH = pl.DeviceIdType.MESH


def position(slot):
    x = lax.axis_index("gx") + (slot // 3 - 1)
    y = lax.axis_index("gy") + (slot % 3 - 1)
    in_x = (x >= 0) & (x < lax.axis_size("gx"))
    in_y = (y >= 0) & (y < lax.axis_size("gy"))
    return x, y, in_x, in_y


def greet(extra):
    barrier = pltpu.get_barrier_semaphore()
    total = jnp.int32(len(extra))
    for slot in (1, 3, 5, 7):
        x, y, in_x, in_y = position(slot)
        inside = in_x & in_y
        total = total + inside.astype(jnp.int32)

        @pl.when(inside)
        def _():
            pl.semaphore_signal(barrier, inc=1, device_id={"gx": x, "gy": y}, device_id_type=MESH)

    for where in extra:
        pl.semaphore_signal(barrier, inc=1, device_id=where, device_id_type=MESH)
    pl.semaphore_wait(barrier, total)


def remote(src, dst, send_sem, recv_sem, where):
    return pltpu.make_async_remote_copy(
        src_ref=src, dst_ref=dst, send_sem=send_sem, recv_sem=recv_sem,
        device_id=where, device_id_type=MESH,
    )


def halo_kernel(own_ref, around_ref, send_sem, recv_sem):
    mine = own_ref[...].astype(jnp.float32).T.astype(jnp.bfloat16)
    around_ref[4] = mine
    for slot in range(9):
        if slot != 4:
            _, _, in_x, in_y = position(slot)

            @pl.when(jnp.logical_not(in_x & in_y))
            def _():
                around_ref[slot] = jnp.zeros(mine.shape, mine.dtype)

    greet([])

    def transfer(slot):
        a, b = slot // 3, slot % 3
        x, y, back_x, back_y = position(8 - slot)
        _, _, in_x, in_y = position(slot)
        if b == 1:
            source, where, sends = 4, {"gx": x}, back_x
        else:
            source, where, sends = 3 * a + 1, {"gy": y}, in_x & back_y
        copy = remote(
            around_ref.at[source], around_ref.at[slot], send_sem.at[slot], recv_sem.at[slot], where
        )
        return copy, sends, in_x & in_y

    copies = {slot: transfer(slot) for slot in range(9) if slot != 4}

    def start(*slots):
        for slot in slots:
            pl.when(copies[slot][1])(copies[slot][0].start)

    def arrived(*slots):
        for slot in slots:
            pl.when(copies[slot][2])(copies[slot][0].wait_recv)

    start(1, 7, 3, 5)
    arrived(1)
    start(0, 2)
    arrived(7)
    start(6, 8)
    arrived(3, 5, 0, 2, 6, 8)
    for copy, sends, _ in copies.values():
        pl.when(sends)(copy.wait_send)


def run_halo(own):
    rows, features = own.shape
    vmem = pl.BlockSpec(memory_space=pltpu.VMEM)
    return pl.pallas_call(
        halo_kernel,
        in_specs=[vmem],
        out_specs=vmem,
        out_shape=jax.ShapeDtypeStruct((9, features, rows), own.dtype),
        scratch_shapes=[
            pltpu.SemaphoreType.DMA((9,)),
            pltpu.SemaphoreType.DMA((9,)),
        ],
        compiler_params=pltpu.CompilerParams(collective_id=0, has_side_effects=True),
    )(own)


def tail_kernel(
    pieces_ref, kept_ref, grads_ref, acc_ref, full_s,
    back_s, pass_s, low_s, sum_s, low2_s, row_s, col_s,
    send_h, recv_h, send_r, recv_r,
):
    f32, b16 = jnp.float32, jnp.bfloat16
    p, q = lax.axis_index("gx"), lax.axis_index("gy")
    nx, ny = lax.axis_size("gx"), lax.axis_size("gy")
    padded, features = grads_ref.shape
    big, small = padded // ny, padded // (nx * ny)
    along_y = [(d, lax.rem(q + d, ny)) for d in range(1, ny)]
    along_x = [(d, lax.rem(p + d, nx)) for d in range(1, nx)]

    low_s[...] = grads_ref[...].astype(b16)
    greet([{"gy": y} for _, y in along_y] + [{"gx": x} for _, x in along_x])

    def rows_of(ref, start, size):
        return ref.at[pl.ds(pl.multiple_of(start, size), size)]

    scatter_y = [
        remote(rows_of(low_s, y * big, big), row_s.at[d], send_r.at[0, d], recv_r.at[0, d], {"gy": y})
        for d, y in along_y
    ]
    for copy in scatter_y:
        copy.start()

    def piece(slot):
        a, b = slot // 3, slot % 3
        x, y, in_x, in_y = position(slot)
        if b == 1:
            landing, source, where = 3 * (2 - a) + 1, pass_s.at[a], {"gx": x}
        else:
            landing, source, where = 3 * a + 2 - b, pieces_ref.at[slot], {"gy": y}
        copy = remote(source, back_s.at[landing], send_h.at[slot], recv_h.at[landing], where)
        return copy, in_x & in_y

    copies = {slot: piece(slot) for slot in range(9) if slot != 4}

    def take(slot):
        @pl.when(copies[slot][1])
        def _():
            x, y, _, _ = position(slot)
            sender = {"gx": x} if slot % 3 == 1 else {"gy": y}
            landed = back_s.at[slot]
            remote(landed, landed, send_h.at[slot], recv_h.at[slot], sender).wait_recv()
            acc_ref[...] += back_s[slot].astype(f32)

    total = grads_ref[pl.ds(pl.multiple_of(q * big, big), big), :]
    for (d, _), copy in zip(along_y, scatter_y):
        copy.wait_recv()
        total = total + row_s[d].astype(f32)
    sum_s[...] = total
    low2_s[...] = total.astype(b16)
    scatter_x = [
        remote(rows_of(low2_s, x * small, small), col_s.at[d], send_r.at[1, d], recv_r.at[1, d], {"gx": x})
        for d, x in along_x
    ]
    for copy in scatter_x:
        copy.start()
    for slot in (0, 2, 6, 8, 3, 5):
        pl.when(copies[slot][1])(copies[slot][0].start)
    total = sum_s[pl.ds(pl.multiple_of(p * small, small), small), :]
    for (d, _), copy in zip(along_x, scatter_x):
        copy.wait_recv()
        total = total + col_s[d].astype(f32)
    own_rows = rows_of(full_s, q * big + p * small, small)
    own_rows[...] = total.astype(b16)
    gather_x = [
        remote(own_rows, own_rows, send_r.at[2, d], recv_r.at[2, d], {"gx": x}) for d, x in along_x
    ]
    for copy in gather_x:
        copy.start()
    for a in (0, 2):
        acc_ref[...] = pieces_ref[3 * a + 1].astype(f32)
        take(3 * a)
        take(3 * a + 2)
        pass_s[a] = acc_ref[...].astype(b16)
        pl.when(copies[3 * a + 1][1])(copies[3 * a + 1][0].start)
    for d, _ in along_x:
        source = lax.rem(p + nx - d, nx)
        theirs = rows_of(full_s, q * big + source * small, small)
        remote(theirs, theirs, send_r.at[2, d], recv_r.at[2, d], {"gx": source}).wait_recv()
    for copy in gather_x:
        copy.wait_send()
    own_big = rows_of(full_s, q * big, big)
    gather_y = [
        remote(own_big, own_big, send_r.at[3, d], recv_r.at[3, d], {"gy": y}) for d, y in along_y
    ]
    for copy in gather_y:
        copy.start()

    acc_ref[...] = kept_ref[...]
    for slot in (3, 5, 1, 7):
        take(slot)
    for d, _ in along_y:
        source = lax.rem(q + ny - d, ny)
        theirs = rows_of(full_s, source * big, big)
        remote(theirs, theirs, send_r.at[3, d], recv_r.at[3, d], {"gy": source}).wait_recv()
    for copy in scatter_y + scatter_x + gather_y:
        copy.wait_send()
    for copy, sends in copies.values():
        pl.when(sends)(copy.wait_send)


def finish_kernel(
    acc_hbm, full_hbm, node_ref, g1_ref, g2_ref, gn1_ref, gn2_ref, acc_ref, full_ref, fetch_sem
):
    fetch_acc = pltpu.make_async_copy(acc_hbm, acc_ref, fetch_sem.at[0])
    fetch_acc.start()
    fetch_full = pltpu.make_async_copy(full_hbm, full_ref, fetch_sem.at[1])
    fetch_full.start()
    fetch_acc.wait()
    fetch_full.wait()
    node_ref[...] = acc_ref[...].T
    first = 0
    for ref in (g1_ref, g2_ref, gn1_ref, gn2_ref):
        ref[...] = full_ref[first : first + ref.shape[0]].astype(jnp.float32)
        first += ref.shape[0]


def run_finish(acc, full):
    features, rows = acc.shape
    vmem = pl.BlockSpec(memory_space=pltpu.VMEM)
    shape = jax.ShapeDtypeStruct
    return pl.pallas_call(
        finish_kernel,
        in_specs=[pl.BlockSpec(memory_space=pl.ANY)] * 2,
        out_specs=[vmem] * 5,
        out_shape=[shape((rows, features), jnp.float32)]
        + [shape((n * features, features), jnp.float32) for n in (3, 1, 2, 1)],
        scratch_shapes=[
            pltpu.VMEM(acc.shape, acc.dtype),
            pltpu.VMEM(full.shape, full.dtype),
            pltpu.SemaphoreType.DMA((2,)),
        ],
        compiler_params=pltpu.CompilerParams(vmem_limit_bytes=60 * 1024 * 1024),
    )(acc, full)


def run_tail(pieces, kept, grads):
    f32, b16 = jnp.float32, jnp.bfloat16
    features, rows = kept.shape
    nx, ny = lax.axis_size("gx"), lax.axis_size("gy")
    padded = grads.shape[0]
    big, small = padded // ny, padded // (nx * ny)
    vmem = pl.BlockSpec(memory_space=pltpu.VMEM)
    shape = jax.ShapeDtypeStruct
    return pl.pallas_call(
        tail_kernel,
        in_specs=[vmem] * 3,
        out_specs=[vmem] * 2,
        out_shape=[shape((features, rows), f32), shape((padded, features), b16)],
        scratch_shapes=[
            pltpu.VMEM((9, features, rows), b16),
            pltpu.VMEM((3, features, rows), b16),
            pltpu.VMEM((padded, features), b16),
            pltpu.VMEM((big, features), f32),
            pltpu.VMEM((big, features), b16),
            pltpu.VMEM((ny, big, features), b16),
            pltpu.VMEM((nx, small, features), b16),
            pltpu.SemaphoreType.DMA((9,)),
            pltpu.SemaphoreType.DMA((9,)),
            pltpu.SemaphoreType.DMA((4, max(nx, ny))),
            pltpu.SemaphoreType.DMA((4, max(nx, ny))),
        ],
        compiler_params=pltpu.CompilerParams(
            collective_id=1, has_side_effects=True, vmem_limit_bytes=32 * 1024 * 1024
        ),
    )(pieces, kept, grads)


def passed_along(value, axis, steps):
    count = lax.axis_size(axis)
    initial, last = (max(0, -steps), min(count, count - steps))
    return lax.ppermute(value, axis, [(source, source + steps) for source in range(initial, last)])


def return_permute(pieces, kept):
    row_span = lax.axis_size("gy")
    row_place = lax.axis_index("gy")
    incoming = kept
    for across in range(3):
        for within in range(3):
            if across != 1 or within != 1:
                shift_gx = across - 1
                shift_gy = within - 1
                arrived = passed_along(
                    pieces[3 * across + within],
                    ("gx", "gy"),
                    shift_gx * row_span + shift_gy,
                ).astype(jnp.float32)
                inside = (row_place - shift_gy >= 0) & (row_place - shift_gy < row_span)
                incoming = incoming + jnp.where(inside, arrived, 0.0)
    return incoming.T


def shards(
    latents, edge_latents, pair_send, pair_count, edge_send, edge_recv,
    edge_w1, edge_w2, node_w1, node_w2, node_ct,
):
    rows, features = latents.shape[2:]
    own = latents[0, 0]
    around = run_halo(own)
    nx, ny = lax.axis_size("gx"), lax.axis_size("gy")
    factor = 1.0 / math.sqrt(rows * nx * ny)
    direct = nx * ny <= 16
    unit = 16 * nx * ny if direct else 1
    padded = -(-7 * features // unit) * unit
    updated, kept, pieces, grads = run_local(
        factor, padded, pair_send[0, 0], pair_count[0], around, edge_latents[0, 0],
        edge_send[0, 0], edge_recv[0, 0], edge_w1, edge_w2, node_w1, node_w2, own, node_ct[0, 0],
    )
    if direct:
        node_grad, *summed = run_finish(*run_tail(pieces, kept, grads))
    else:
        node_grad = return_permute(pieces, kept)
        grads = lax.psum(grads, ("gx", "gy"))
        summed = jnp.split(grads, (3 * features, 4 * features, 6 * features))
    return (updated[None, None], node_grad[None, None]) + tuple(summed)


def solution(mesh):
    block = P(("grp", "gx"), "gy")
    return jax.shard_map(
        shards,
        mesh=mesh,
        in_specs=(block,) * 6 + (P(),) * 4 + (block,),
        out_specs=(block, block) + (P("grp", None),) * 4,
        check_vma=False,
    )
```

```python
import functools
import math

import jax
import jax.numpy as jnp
from jax import lax
from jax.experimental import pallas as pl
from jax.experimental.pallas import tpu as pltpu
from jax.sharding import PartitionSpec as P

EPSILON = 1e-05
UNROLL = 6


def nn(a, b):
    return lax.dot_general(a, b, (((1,), (0,)), ((), ())), preferred_element_type=jnp.float32)


def nt(a, b):
    return lax.dot_general(a, b, (((1,), (1,)), ((), ())), preferred_element_type=jnp.float32)


def moments(values):
    centre = jnp.mean(values, axis=0, keepdims=True)
    shifted = values - centre
    inverse_std = lax.rsqrt(jnp.mean(shifted * shifted, axis=0, keepdims=True) + EPSILON)
    return shifted * inverse_std, inverse_std


def norm_back(normed, inverse_std, upstream):
    return inverse_std * (
        upstream
        - jnp.mean(upstream, axis=0, keepdims=True)
        - normed * jnp.mean(upstream * normed, axis=0, keepdims=True)
    )


def local_kernel(
    factor, send_ref, count_ref, around_hbm, edges_hbm, sidx_ref, ridx_ref,
    w1_ref, w2_ref, nw1_ref, nw2_ref, own_ref, ct_ref,
    out_ref, self_ref, piece_ref, grads_ref,
    slope_s, act_s, hat_s, inv_s, w1t_s, agg_s, gagg_s, gr_s, gs_s, g1a_s, g2_s,
    around_ref, edges_ref, fetch_sem,
):
    f32, b16 = jnp.float32, jnp.bfloat16
    fetch_around = pltpu.make_async_copy(around_hbm, around_ref, fetch_sem.at[0])
    fetch_around.start()
    fetch_edges = pltpu.make_async_copy(edges_hbm, edges_ref, fetch_sem.at[1])
    fetch_edges.start()
    slots, width = sidx_ref.shape
    features, rows = around_ref.shape[1:]
    count = count_ref[0]
    steps = lax.div(count + (UNROLL - 1), UNROLL)

    w1t_s[...] = w1_ref[...].astype(f32).T.astype(b16)
    w2t = w2_ref[...].astype(f32).T.astype(b16)
    agg_s[...] = jnp.zeros_like(agg_s)
    gr_s[...] = jnp.zeros_like(gr_s)
    gs_s[...] = jnp.zeros_like(gs_s)
    g1a_s[...] = jnp.zeros_like(g1a_s)
    g2_s[...] = jnp.zeros_like(g2_s)
    fetch_around.wait()
    fetch_edges.wait()

    def place(index_ref, step, limit):
        parts = []
        for u in range(UNROLL):
            k = step * UNROLL + u
            index = index_ref[pl.ds(k, 1), :]
            if limit:
                index = jnp.where(k < count, index, rows)
            parts.append(index)
        index = jnp.concatenate(parts, axis=1)
        spot = lax.broadcasted_iota(jnp.int16, (rows, UNROLL * width), 0)
        match = spot == index.astype(jnp.int16)
        return jnp.where(match, jnp.ones((), b16), jnp.zeros((), b16))

    def forward(step, carry):
        at_recv = place(ridx_ref, step, True)
        at_send = place(sidx_ref, step, False)
        receivers = nn(around_ref[4], at_recv).astype(b16)
        senders = jnp.concatenate(
            [
                nn(
                    around_ref[send_ref[step * UNROLL + u]],
                    at_send[:, u * width : (u + 1) * width],
                ).astype(b16)
                for u in range(UNROLL)
            ],
            axis=1,
        )
        edge = edges_ref[pl.ds(step * UNROLL, UNROLL)].reshape(UNROLL * width, features)
        pre = nt(w1t_s[:, :features], edge) + nn(
            w1t_s[:, features:], jnp.concatenate([receivers, senders], axis=0)
        )
        sigmoid = 1.0 / (1.0 + jnp.exp(-pre))
        act = (pre * sigmoid).astype(b16)
        slope_s[step] = sigmoid * (1.0 + pre * (1.0 - sigmoid))
        act_s[step] = act
        normed, inverse_std = moments(nn(w2t, act))
        hat_s[step] = normed
        inv_s[step] = inverse_std
        agg_s[...] += nt(normed.astype(b16), at_recv)
        return carry

    lax.fori_loop(0, steps, forward, 0)

    own = around_ref[4]
    stacked = jnp.concatenate([own, agg_s[...].astype(b16)], axis=0)
    nw1t = nw1_ref[...].astype(f32).T.astype(b16)
    nw2t = nw2_ref[...].astype(f32).T.astype(b16)
    pre = nn(nw1t, stacked)
    sigmoid = 1.0 / (1.0 + jnp.exp(-pre))
    act = (pre * sigmoid).astype(b16)
    slope = sigmoid * (1.0 + pre * (1.0 - sigmoid))
    normed, inverse_std = moments(nn(nw2t, act))
    out_ref[...] = (own_ref[...].astype(f32) + normed.T).astype(b16)
    upstream = ct_ref[...].astype(f32).T
    grad_second = norm_back(normed, inverse_std, upstream).astype(b16)
    grads_ref[6 * features : 7 * features] = nt(act, grad_second) * factor
    grad_first = (nn(nw2_ref[...], grad_second) * slope).astype(b16)
    grads_ref[4 * features : 6 * features] = nt(stacked, grad_first) * factor
    grad_inputs = nn(nw1_ref[...], grad_first)
    self_ref[...] = upstream + grad_inputs[:features]
    gagg_s[...] = grad_inputs[features:].astype(b16)

    def backward(step, carry):
        at_recv = place(ridx_ref, step, True)
        at_send = place(sidx_ref, step, False)
        upstream = nn(gagg_s[...], at_recv)
        act = act_s[step]
        grad_second = norm_back(hat_s[step], inv_s[step], upstream).astype(b16)
        g2_s[...] += nt(act, grad_second)
        grad_first = (nn(w2_ref[...], grad_second) * slope_s[step]).astype(b16)
        edge = edges_ref[pl.ds(step * UNROLL, UNROLL)].reshape(UNROLL * width, features)
        g1a_s[...] += nn(grad_first, edge)
        gr_s[...] += nt(grad_first, at_recv)
        for u in range(UNROLL):
            part = slice(u * width, (u + 1) * width)
            gs_s[send_ref[step * UNROLL + u]] += nt(grad_first[:, part], at_send[:, part])
        return carry

    lax.fori_loop(0, steps, backward, 0)

    to_recv = gr_s[...].astype(b16)
    grads_ref[:features] = g1a_s[...].T * factor
    grads_ref[features : 2 * features] = nt(own, to_recv) * factor
    self_ref[...] += nn(w1_ref[features : 2 * features], to_recv)
    total = jnp.zeros((features, features), f32)
    for b in range(9):
        to_send = gs_s[b].astype(b16)
        total += nt(around_ref[b], to_send)
        piece_ref[b] = nn(w1_ref[2 * features :], to_send).astype(b16)
    grads_ref[2 * features : 3 * features] = total * factor
    grads_ref[3 * features : 4 * features] = g2_s[...] * factor
    if grads_ref.shape[0] > 7 * features:
        grads_ref[7 * features :] = jnp.zeros((grads_ref.shape[0] - 7 * features, features), f32)
    self_ref[...] += nn(w1_ref[2 * features :], gs_s[4].astype(b16))


def run_local(factor, padded, send, count, around, edges, sidx, ridx, w1, w2, nw1, nw2, own, ct):
    f32, b16 = jnp.float32, jnp.bfloat16
    rows, features = own.shape
    slots, width = sidx.shape
    steps = slots // UNROLL
    wide = UNROLL * width
    smem = pl.BlockSpec(memory_space=pltpu.SMEM)
    vmem = pl.BlockSpec(memory_space=pltpu.VMEM)
    shape = jax.ShapeDtypeStruct
    return pl.pallas_call(
        functools.partial(local_kernel, factor),
        in_specs=[smem, smem] + [pl.BlockSpec(memory_space=pl.ANY)] * 2 + [vmem] * 8,
        out_specs=[vmem] * 4,
        out_shape=[
            shape((rows, features), b16),
            shape((features, rows), f32),
            shape((9, features, rows), b16),
            shape((padded, features), f32),
        ],
        scratch_shapes=[
            pltpu.VMEM((steps, features, wide), f32),
            pltpu.VMEM((steps, features, wide), b16),
            pltpu.VMEM((steps, features, wide), f32),
            pltpu.VMEM((steps, 1, wide), f32),
            pltpu.VMEM((features, 3 * features), b16),
            pltpu.VMEM((features, rows), f32),
            pltpu.VMEM((features, rows), b16),
            pltpu.VMEM((features, rows), f32),
            pltpu.VMEM((9, features, rows), f32),
            pltpu.VMEM((features, features), f32),
            pltpu.VMEM((features, features), f32),
            pltpu.VMEM(around.shape, b16),
            pltpu.VMEM(edges.shape, b16),
            pltpu.SemaphoreType.DMA((2,)),
        ],
        compiler_params=pltpu.CompilerParams(vmem_limit_bytes=60 * 1024 * 1024),
    )(send, count, around, edges, sidx, ridx, w1, w2, nw1, nw2, own, ct)


MESH = pl.DeviceIdType.MESH


def position(slot):
    x = lax.axis_index("gx") + (slot // 3 - 1)
    y = lax.axis_index("gy") + (slot % 3 - 1)
    in_x = (x >= 0) & (x < lax.axis_size("gx"))
    in_y = (y >= 0) & (y < lax.axis_size("gy"))
    return x, y, in_x, in_y


def greet(extra):
    barrier = pltpu.get_barrier_semaphore()
    total = jnp.int32(len(extra))
    for slot in (1, 3, 5, 7):
        x, y, in_x, in_y = position(slot)
        inside = in_x & in_y
        total = total + inside.astype(jnp.int32)

        @pl.when(inside)
        def _():
            pl.semaphore_signal(barrier, inc=1, device_id={"gx": x, "gy": y}, device_id_type=MESH)

    for where in extra:
        pl.semaphore_signal(barrier, inc=1, device_id=where, device_id_type=MESH)
    pl.semaphore_wait(barrier, total)


def remote(src, dst, send_sem, recv_sem, where):
    return pltpu.make_async_remote_copy(
        src_ref=src, dst_ref=dst, send_sem=send_sem, recv_sem=recv_sem,
        device_id=where, device_id_type=MESH,
    )


def halo_kernel(own_ref, around_ref, send_sem, recv_sem):
    mine = own_ref[...].astype(jnp.float32).T.astype(jnp.bfloat16)
    around_ref[4] = mine
    for slot in range(9):
        if slot != 4:
            _, _, in_x, in_y = position(slot)

            @pl.when(jnp.logical_not(in_x & in_y))
            def _():
                around_ref[slot] = jnp.zeros(mine.shape, mine.dtype)

    greet([])

    def transfer(slot):
        a, b = slot // 3, slot % 3
        x, y, back_x, back_y = position(8 - slot)
        _, _, in_x, in_y = position(slot)
        if b == 1:
            source, where, sends = 4, {"gx": x}, back_x
        else:
            source, where, sends = 3 * a + 1, {"gy": y}, in_x & back_y
        copy = remote(
            around_ref.at[source], around_ref.at[slot], send_sem.at[slot], recv_sem.at[slot], where
        )
        return copy, sends, in_x & in_y

    copies = {slot: transfer(slot) for slot in range(9) if slot != 4}

    def start(*slots):
        for slot in slots:
            pl.when(copies[slot][1])(copies[slot][0].start)

    def arrived(*slots):
        for slot in slots:
            pl.when(copies[slot][2])(copies[slot][0].wait_recv)

    start(1, 7, 3, 5)
    arrived(1)
    start(0, 2)
    arrived(7)
    start(6, 8)
    arrived(3, 5, 0, 2, 6, 8)
    for copy, sends, _ in copies.values():
        pl.when(sends)(copy.wait_send)


def run_halo(own):
    rows, features = own.shape
    vmem = pl.BlockSpec(memory_space=pltpu.VMEM)
    return pl.pallas_call(
        halo_kernel,
        in_specs=[vmem],
        out_specs=vmem,
        out_shape=jax.ShapeDtypeStruct((9, features, rows), own.dtype),
        scratch_shapes=[
            pltpu.SemaphoreType.DMA((9,)),
            pltpu.SemaphoreType.DMA((9,)),
        ],
        compiler_params=pltpu.CompilerParams(collective_id=0, has_side_effects=True),
    )(own)


def tail_kernel(
    pieces_ref, kept_hbm, grads_hbm, acc_ref, full_s,
    back_s, pass_s, low_s, sum_s, low2_s, row_s, col_s,
    send_h, recv_h, send_r, recv_r, kept_ref, grads_ref, middle_s, fetch_sem,
):
    fetch_grads = pltpu.make_async_copy(grads_hbm, grads_ref, fetch_sem.at[0])
    fetch_grads.start()
    fetches = [
        pltpu.make_async_copy(kept_hbm, kept_ref, fetch_sem.at[1]),
        pltpu.make_async_copy(pieces_ref.at[1], middle_s.at[0], fetch_sem.at[2]),
        pltpu.make_async_copy(pieces_ref.at[7], middle_s.at[2], fetch_sem.at[3]),
    ]
    for fetch in fetches:
        fetch.start()
    f32, b16 = jnp.float32, jnp.bfloat16
    p, q = lax.axis_index("gx"), lax.axis_index("gy")
    nx, ny = lax.axis_size("gx"), lax.axis_size("gy")
    padded, features = grads_hbm.shape
    big, small = padded // ny, padded // (nx * ny)
    along_y = [(d, lax.rem(q + d, ny)) for d in range(1, ny)]
    along_x = [(d, lax.rem(p + d, nx)) for d in range(1, nx)]

    fetch_grads.wait()
    low_s[...] = grads_ref[...].astype(b16)
    greet([{"gy": y} for _, y in along_y] + [{"gx": x} for _, x in along_x])

    def rows_of(ref, start, size):
        return ref.at[pl.ds(pl.multiple_of(start, size), size)]

    scatter_y = [
        remote(rows_of(low_s, y * big, big), row_s.at[d], send_r.at[0, d], recv_r.at[0, d], {"gy": y})
        for d, y in along_y
    ]
    for copy in scatter_y:
        copy.start()

    def piece(slot):
        a, b = slot // 3, slot % 3
        x, y, in_x, in_y = position(slot)
        if b == 1:
            landing, source, where = 3 * (2 - a) + 1, pass_s.at[a], {"gx": x}
        else:
            landing, source, where = 3 * a + 2 - b, pieces_ref.at[slot], {"gy": y}
        copy = remote(source, back_s.at[landing], send_h.at[slot], recv_h.at[landing], where)
        return copy, in_x & in_y

    copies = {slot: piece(slot) for slot in range(9) if slot != 4}

    def take(slot):
        @pl.when(copies[slot][1])
        def _():
            x, y, _, _ = position(slot)
            sender = {"gx": x} if slot % 3 == 1 else {"gy": y}
            landed = back_s.at[slot]
            remote(landed, landed, send_h.at[slot], recv_h.at[slot], sender).wait_recv()
            acc_ref[...] += back_s[slot].astype(f32)

    total = grads_ref[pl.ds(pl.multiple_of(q * big, big), big), :]
    for (d, _), copy in zip(along_y, scatter_y):
        copy.wait_recv()
        total = total + row_s[d].astype(f32)
    sum_s[...] = total
    low2_s[...] = total.astype(b16)
    scatter_x = [
        remote(rows_of(low2_s, x * small, small), col_s.at[d], send_r.at[1, d], recv_r.at[1, d], {"gx": x})
        for d, x in along_x
    ]
    for copy in scatter_x:
        copy.start()
    for slot in (0, 2, 6, 8, 3, 5):
        pl.when(copies[slot][1])(copies[slot][0].start)
    total = sum_s[pl.ds(pl.multiple_of(p * small, small), small), :]
    for (d, _), copy in zip(along_x, scatter_x):
        copy.wait_recv()
        total = total + col_s[d].astype(f32)
    own_rows = rows_of(full_s, q * big + p * small, small)
    own_rows[...] = total.astype(b16)
    gather_x = [
        remote(own_rows, own_rows, send_r.at[2, d], recv_r.at[2, d], {"gx": x}) for d, x in along_x
    ]
    for copy in gather_x:
        copy.start()
    for fetch in fetches:
        fetch.wait()
    for a in (0, 2):
        acc_ref[...] = middle_s[a].astype(f32)
        take(3 * a)
        take(3 * a + 2)
        pass_s[a] = acc_ref[...].astype(b16)
        pl.when(copies[3 * a + 1][1])(copies[3 * a + 1][0].start)
    for d, _ in along_x:
        source = lax.rem(p + nx - d, nx)
        theirs = rows_of(full_s, q * big + source * small, small)
        remote(theirs, theirs, send_r.at[2, d], recv_r.at[2, d], {"gx": source}).wait_recv()
    for copy in gather_x:
        copy.wait_send()
    own_big = rows_of(full_s, q * big, big)
    gather_y = [
        remote(own_big, own_big, send_r.at[3, d], recv_r.at[3, d], {"gy": y}) for d, y in along_y
    ]
    for copy in gather_y:
        copy.start()

    acc_ref[...] = kept_ref[...]
    for slot in (3, 5, 1, 7):
        take(slot)
    for d, _ in along_y:
        source = lax.rem(q + ny - d, ny)
        theirs = rows_of(full_s, source * big, big)
        remote(theirs, theirs, send_r.at[3, d], recv_r.at[3, d], {"gy": source}).wait_recv()
    for copy in scatter_y + scatter_x + gather_y:
        copy.wait_send()
    for copy, sends in copies.values():
        pl.when(sends)(copy.wait_send)


def finish_kernel(
    acc_hbm, full_hbm, node_ref, g1_ref, g2_ref, gn1_ref, gn2_ref, acc_ref, full_ref, fetch_sem
):
    fetch_acc = pltpu.make_async_copy(acc_hbm, acc_ref, fetch_sem.at[0])
    fetch_acc.start()
    fetch_full = pltpu.make_async_copy(full_hbm, full_ref, fetch_sem.at[1])
    fetch_full.start()
    fetch_acc.wait()
    fetch_full.wait()
    node_ref[...] = acc_ref[...].T
    first = 0
    for ref in (g1_ref, g2_ref, gn1_ref, gn2_ref):
        ref[...] = full_ref[first : first + ref.shape[0]].astype(jnp.float32)
        first += ref.shape[0]


def run_finish(acc, full):
    features, rows = acc.shape
    vmem = pl.BlockSpec(memory_space=pltpu.VMEM)
    shape = jax.ShapeDtypeStruct
    return pl.pallas_call(
        finish_kernel,
        in_specs=[pl.BlockSpec(memory_space=pl.ANY)] * 2,
        out_specs=[vmem] * 5,
        out_shape=[shape((rows, features), jnp.float32)]
        + [shape((n * features, features), jnp.float32) for n in (3, 1, 2, 1)],
        scratch_shapes=[
            pltpu.VMEM(acc.shape, acc.dtype),
            pltpu.VMEM(full.shape, full.dtype),
            pltpu.SemaphoreType.DMA((2,)),
        ],
        compiler_params=pltpu.CompilerParams(vmem_limit_bytes=60 * 1024 * 1024),
    )(acc, full)


def run_tail(pieces, kept, grads):
    f32, b16 = jnp.float32, jnp.bfloat16
    features, rows = kept.shape
    nx, ny = lax.axis_size("gx"), lax.axis_size("gy")
    padded = grads.shape[0]
    big, small = padded // ny, padded // (nx * ny)
    vmem = pl.BlockSpec(memory_space=pltpu.VMEM)
    shape = jax.ShapeDtypeStruct
    return pl.pallas_call(
        tail_kernel,
        in_specs=[pl.BlockSpec(memory_space=pl.ANY)] * 3,
        out_specs=[vmem] * 2,
        out_shape=[shape((features, rows), f32), shape((padded, features), b16)],
        scratch_shapes=[
            pltpu.VMEM((9, features, rows), b16),
            pltpu.VMEM((3, features, rows), b16),
            pltpu.VMEM((padded, features), b16),
            pltpu.VMEM((big, features), f32),
            pltpu.VMEM((big, features), b16),
            pltpu.VMEM((ny, big, features), b16),
            pltpu.VMEM((nx, small, features), b16),
            pltpu.SemaphoreType.DMA((9,)),
            pltpu.SemaphoreType.DMA((9,)),
            pltpu.SemaphoreType.DMA((4, max(nx, ny))),
            pltpu.SemaphoreType.DMA((4, max(nx, ny))),
            pltpu.VMEM((features, rows), f32),
            pltpu.VMEM((padded, features), f32),
            pltpu.VMEM((3, features, rows), b16),
            pltpu.SemaphoreType.DMA((4,)),
        ],
        compiler_params=pltpu.CompilerParams(
            collective_id=1, has_side_effects=True, vmem_limit_bytes=63 * 1024 * 1024
        ),
    )(pieces, kept, grads)


def passed_along(value, axis, steps):
    count = lax.axis_size(axis)
    initial, last = (max(0, -steps), min(count, count - steps))
    return lax.ppermute(value, axis, [(source, source + steps) for source in range(initial, last)])


def return_permute(pieces, kept):
    row_span = lax.axis_size("gy")
    row_place = lax.axis_index("gy")
    incoming = kept
    for across in range(3):
        for within in range(3):
            if across != 1 or within != 1:
                shift_gx = across - 1
                shift_gy = within - 1
                arrived = passed_along(
                    pieces[3 * across + within],
                    ("gx", "gy"),
                    shift_gx * row_span + shift_gy,
                ).astype(jnp.float32)
                inside = (row_place - shift_gy >= 0) & (row_place - shift_gy < row_span)
                incoming = incoming + jnp.where(inside, arrived, 0.0)
    return incoming.T


def shards(
    latents, edge_latents, pair_send, pair_count, edge_send, edge_recv,
    edge_w1, edge_w2, node_w1, node_w2, node_ct,
):
    rows, features = latents.shape[2:]
    own = latents[0, 0]
    around = run_halo(own)
    nx, ny = lax.axis_size("gx"), lax.axis_size("gy")
    factor = 1.0 / math.sqrt(rows * nx * ny)
    direct = nx * ny <= 16
    unit = 16 * nx * ny if direct else 1
    padded = -(-7 * features // unit) * unit
    updated, kept, pieces, grads = run_local(
        factor, padded, pair_send[0, 0], pair_count[0], around, edge_latents[0, 0],
        edge_send[0, 0], edge_recv[0, 0], edge_w1, edge_w2, node_w1, node_w2, own, node_ct[0, 0],
    )
    if direct:
        node_grad, *summed = run_finish(*run_tail(pieces, kept, grads))
    else:
        node_grad = return_permute(pieces, kept)
        grads = lax.psum(grads, ("gx", "gy"))
        summed = jnp.split(grads, (3 * features, 4 * features, 6 * features))
    return (updated[None, None], node_grad[None, None]) + tuple(summed)


def solution(mesh):
    block = P(("grp", "gx"), "gy")
    return jax.shard_map(
        shards,
        mesh=mesh,
        in_specs=(block,) * 6 + (P(),) * 4 + (block,),
        out_specs=(block, block) + (P("grp", None),) * 4,
        check_vma=False,
    )
```
